32 devices in a mesh: seq: 8 (over z, x), head: 4 (over y, core).
Axes of the slice: x: 2, y: 2, z: 4, core: 2. Of those that a mesh axis runs over, the one named last changes fastest.
Arguments:
- query_rows: bfloat16 [4096, 4096], P(('seq', 'head')), may hold values from -6 to 6
- key_rows: bfloat16 [4096, 4096], P(('seq', 'head')), may hold values from -6 to 6
- value_rows: bfloat16 [4096, 4096], P(('seq', 'head')), may hold values from -6 to 6
- residual: bfloat16 [4096, 5120], P('seq', 'head'), may hold values from -6 to 6
- out_weight: bfloat16 [4096, 5120], P(None, 'head'), may hold values from -0.09375 to 0.09375
- proj_first: bfloat16 [5120, 1024], P('head'), may hold values from -0.078125 to 0.078125
- proj_second: bfloat16 [1024, 1536], replicated, may hold values from -0.1875 to 0.1875
- dino_feats: bfloat16 [16, 64, 1536], P('seq', 'head'), may hold values from -60 to 60
- slot_frame: int32 [16], replicated, may hold values from 0 to 15, as said below
- patch_taps: int32 [4096, 4], P(('seq', 'head')), may hold values from 0 to 63
Outputs:
- hidden: bfloat16 [4096, 5120], P('seq', 'head')
- projected: bfloat16 [4096, 1536], P(('seq', 'head'))
- target: float32 [4096, 1536], P(('seq', 'head'))
- cosine: float32 [4096], P(('seq', 'head'))
The draws below stay inside these ranges and needn't reach their ends.
Inputs may be any that keep to these rules, and one draw needn't show every extreme that they name: slot_frame is a permutation of the frames; the 2 slots of one seq index (slots i * 2 to (i + 1) * 2 - 1) hold frames of 2 different seq indices' tokens, where frames i * 2 to (i + 1) * 2 - 1 are those of seq index i's tokens.
All inputs are finite; a program needn't handle non-finite values.
Results may differ from the reference program's by a relative error of at most 0.0061.
Values may be sent and summed in bfloat16 or wider, within the bound.
A program may use at most 128 MiB of HBM per device.

```python
import math
import jax
import jax.numpy as jnp
from jax import lax

D = 5120
H = 32
HD = 128
Z = 1536
PH = 1024
PPF = 64
TAPS = 4
BLOCK = 512
TOKENS = 4096
TPF = 256
FPB = 2
FRAMES = 16
N_SEQ = 8


def draw_query_rows(key, part):
    own_key = jax.random.fold_in(key, 3)
    values = jnp.clip(1.6 * jax.random.normal(own_key, (TOKENS, H * HD), jnp.float32), -6.0, 6.0)
    return values.astype(jnp.bfloat16)


def draw_key_rows(key, part):
    own_key = jax.random.fold_in(key, 4)
    values = jnp.clip(1.6 * jax.random.normal(own_key, (TOKENS, H * HD), jnp.float32), -6.0, 6.0)
    return values.astype(jnp.bfloat16)


def draw_dino_feats(key, part):
    own_key = jax.random.fold_in(key, 5)
    row_key, col_key, main_key = jax.random.split(own_key, 3)
    row_scale = jnp.exp(jax.random.uniform(row_key, (FRAMES, PPF, 1), jnp.float32, 0.0, math.log(10.0))) / math.sqrt(10.0)
    col_scale = jnp.exp(jax.random.uniform(col_key, (1, 1, Z), jnp.float32, 0.0, math.log(10.0))) / math.sqrt(10.0)
    values = jnp.clip(jax.random.normal(main_key, (FRAMES, PPF, Z), jnp.float32), -4.0, 4.0) * row_scale * col_scale
    return values.astype(jnp.bfloat16)


def draw_slot_frame(key, part):
    own_key = jax.random.fold_in(key, 11)
    shift_key, order_key, owner_key, target_key = jax.random.split(own_key, 4)
    shifts = jax.random.permutation(shift_key, N_SEQ).astype(jnp.int32)[:FPB]
    owner_label = jax.random.permutation(owner_key, N_SEQ).astype(jnp.int32)
    target_label = jax.random.permutation(target_key, N_SEQ).astype(jnp.int32)
    within = jax.random.permutation(order_key, FPB).astype(jnp.int32)
    targets = target_label[(owner_label[:, None] + shifts[None, :]) % N_SEQ]
    frames = targets * FPB + within[None, :]
    return frames.reshape(FRAMES).astype(jnp.int32)


def touch_ends(entries, key, least, top_value):
    place = [jax.random.randint(jax.random.fold_in(key, axis), (), 0, length) for axis, length in enumerate(entries.shape)]
    longest = entries.shape.index(max(entries.shape))
    neighbour = place[:longest] + [(place[longest] + 1) % entries.shape[longest]] + place[longest + 1:]
    return entries.at[tuple(place)].set(least).at[tuple(neighbour)].set(top_value)


def steps_of(key, extent, cuts, low, top_value):
    gain = 1.0
    for position, parts in cuts:
        steps = jax.random.uniform(jax.random.fold_in(jax.random.fold_in(key, 6), position), (parts,), jnp.float32, low / len(cuts), top_value / len(cuts))
        gain = gain * jnp.repeat(jnp.exp(steps), extent[position] // parts).reshape((-1,) + (1,) * (len(extent) - 1 - position))
    return gain


def scatter_about(rng, dims, spread, most, pieces=(), held_as=jnp.bfloat16):
    result = spread * jax.random.normal(rng, dims, jnp.float32)
    if pieces:
        result = result * steps_of(rng, dims, pieces, -0.22, 0.18)
    return jnp.clip(result, -most, most).astype(held_as)


def setup_inputs(seed: int = 0) -> dict:
    keys = jax.random.split(jax.random.key(seed), 11)
    query_rows = draw_query_rows(jax.random.fold_in(keys[10], 71), 0)
    key_rows = draw_key_rows(jax.random.fold_in(keys[10], 71), 0)
    value_rows = scatter_about(keys[2], (TOKENS, H * HD), 1.0, 6.0, ((0, 32),))
    residual = scatter_about(keys[3], (TOKENS, D), 1.0, 6.0, ((0, 8), (1, 4)))
    out_weight = scatter_about(keys[4], (H * HD, D), (H * HD) ** -0.5, 0.09375, ((1, 4),))
    proj_first = scatter_about(keys[5], (D, PH), D ** -0.5, 0.078125, ((0, 4),))
    proj_second = scatter_about(keys[6], (PH, Z), PH ** -0.5, 0.1875)
    dino_feats = draw_dino_feats(jax.random.fold_in(keys[10], 71), 0)
    slot_frame = draw_slot_frame(jax.random.fold_in(keys[10], 71), 0)
    patch_taps = touch_ends(jax.random.randint(keys[9], (TOKENS, TAPS), 0, PPF), jax.random.fold_in(keys[9], 1), 0, PPF - 1).astype(jnp.int32)
    return {"query_rows": query_rows, "key_rows": key_rows, "value_rows": value_rows, "residual": residual, "out_weight": out_weight, "proj_first": proj_first, "proj_second": proj_second, "dino_feats": dino_feats, "slot_frame": slot_frame, "patch_taps": patch_taps}


def attend_head(operands):
    query_head, key_head, value_head = operands
    scores = jnp.dot(query_head, key_head.T, preferred_element_type=jnp.float32) * HD ** (-0.5)
    row_max = lax.optimization_barrier(jnp.max(scores, axis=-1, keepdims=True))
    exponents = jnp.exp(scores - row_max)
    weights = (exponents / lax.optimization_barrier(jnp.sum(exponents, axis=-1, keepdims=True))).astype(jnp.bfloat16)
    return jnp.dot(weights, value_head, preferred_element_type=jnp.float32).astype(jnp.bfloat16)

def reference(query_rows, key_rows, value_rows, residual, out_weight, proj_first, proj_second, dino_feats, slot_frame, patch_taps):
    block_count = TOKENS // BLOCK

    def per_block(operands):
        query_block, key_block, value_block, stream_block = operands
        split_heads = (query_block.reshape(BLOCK, H, HD).transpose(1, 0, 2), key_block.reshape(BLOCK, H, HD).transpose(1, 0, 2), value_block.reshape(BLOCK, H, HD).transpose(1, 0, 2))
        attended = lax.map(attend_head, split_heads).transpose(1, 0, 2).reshape(BLOCK, H * HD)
        mixed_sum = jnp.dot(attended, out_weight, preferred_element_type=jnp.float32)
        hidden_block = (stream_block.astype(jnp.float32) + mixed_sum).astype(jnp.bfloat16)
        pre_act = jnp.dot(hidden_block, proj_first, preferred_element_type=jnp.float32)
        lifted = jax.nn.silu(pre_act).astype(jnp.bfloat16)
        projected_block = jnp.dot(lifted, proj_second, preferred_element_type=jnp.float32).astype(jnp.bfloat16)
        return (hidden_block, projected_block)
    hidden, projected = lax.map(per_block, (query_rows.reshape(block_count, BLOCK, H * HD), key_rows.reshape(block_count, BLOCK, H * HD), value_rows.reshape(block_count, BLOCK, H * HD), residual.reshape(block_count, BLOCK, D)))
    hidden = hidden.reshape(TOKENS, D)
    projected = projected.reshape(TOKENS, Z)
    inverse = jnp.zeros((FRAMES,), jnp.int32).at[slot_frame].set(jnp.arange(FRAMES, dtype=jnp.int32))
    ordered = dino_feats[inverse].reshape(FRAMES * PPF, Z)
    frame_of = (jnp.arange(TOKENS, dtype=jnp.int32) // TPF).astype(jnp.int32)
    target = jnp.zeros((TOKENS, Z), jnp.float32)
    for which in range(TAPS):
        target = target + ordered[frame_of * PPF + patch_taps[:, which]].astype(jnp.float32)
    target = target * (1.0 / TAPS)
    proj_float = projected.astype(jnp.float32)
    inner = lax.optimization_barrier(jnp.sum(proj_float * target, axis=-1))
    proj_sq = lax.optimization_barrier(jnp.sum(proj_float * proj_float, axis=-1)) + 1e-06
    target_sq = lax.optimization_barrier(jnp.sum(target * target, axis=-1)) + 1e-06
    cosine = inner / jnp.sqrt(proj_sq * target_sq)
    return (hidden, projected, target, cosine)
```

```python
import functools

import jax
import jax.numpy as jnp
from jax import lax
from jax.experimental import pallas as pl
from jax.experimental.pallas import tpu as pltpu
from jax.sharding import PartitionSpec as P

HD = 128
PPF = 64
TAPS = 4
BLOCK = 512


def attend(operands):
    query_part, key_part, value_part = operands
    length = query_part.shape[0]
    item_count = query_part.shape[2]
    window_count = length // BLOCK
    score_scale = HD ** (-0.5)
    shaped = (
        query_part[:, 0].reshape(window_count, BLOCK, item_count, HD),
        key_part[:, 0].reshape(window_count, BLOCK, item_count, HD),
        value_part[:, 0].reshape(window_count, BLOCK, item_count, HD),
    )

    def one_window(parts):
        query_block, key_block, value_block = parts
        scores = (
            jnp.einsum("qhd,khd->hqk", query_block, key_block, preferred_element_type=jnp.float32)
            * score_scale
        )
        row_max = jnp.max(scores, axis=-1, keepdims=True)
        exponents = jnp.exp(scores - row_max)
        weights = (exponents / jnp.sum(exponents, axis=-1, keepdims=True)).astype(jnp.bfloat16)
        return jnp.einsum(
            "hqk,khd->qhd", weights, value_block, preferred_element_type=jnp.float32
        ).astype(jnp.bfloat16)

    return lax.map(one_window, shaped).reshape(length, 1, item_count, HD)


def per_device(
    query_rows,
    key_rows,
    value_rows,
    residual,
    out_weight,
    proj_first,
    proj_second,
    dino_feats,
    slot_frame,
    patch_taps,
):
    own_rows = query_rows.shape[0]
    group_count = lax.axis_size("head")
    per_group = query_rows.shape[1] // (HD * group_count)
    query_heads = query_rows.reshape(own_rows, group_count, per_group, HD)
    key_heads = key_rows.reshape(own_rows, group_count, per_group, HD)
    value_heads = value_rows.reshape(own_rows, group_count, per_group, HD)
    attended = attend(
        (
            lax.all_to_all(query_heads, "head", split_axis=1, concat_axis=0, tiled=True),
            lax.all_to_all(key_heads, "head", split_axis=1, concat_axis=0, tiled=True),
            lax.all_to_all(value_heads, "head", split_axis=1, concat_axis=0, tiled=True),
        )
    )
    seq_len = attended.shape[0]
    attended = attended.reshape(seq_len, per_group * HD)
    mixed_sum = jnp.dot(
        lax.all_gather(attended, "head", axis=1, tiled=True),
        out_weight,
        preferred_element_type=jnp.float32,
    )
    hidden = (residual.astype(jnp.float32) + mixed_sum).astype(jnp.bfloat16)
    pre_act = lax.psum_scatter(
        jnp.dot(hidden, proj_first, preferred_element_type=jnp.float32),
        "head",
        scatter_dimension=0,
        tiled=True,
    )
    lifted = jax.nn.silu(pre_act).astype(jnp.bfloat16)
    projected = jnp.dot(lifted, proj_second, preferred_element_type=jnp.float32).astype(
        jnp.bfloat16
    )
    seq_index = lax.axis_index("seq")
    head_index = lax.axis_index("head")
    frames_here = dino_feats.shape[0]
    wanted = seq_index * frames_here + jnp.arange(frames_here, dtype=jnp.int32)
    everything = lax.all_gather(dino_feats, "seq", axis=0, tiled=True)
    picker = (slot_frame[None, :] == wanted[:, None]).astype(jnp.bfloat16)
    frame_part = jnp.einsum(
        "ir,rpz->ipz", picker, everything, preferred_element_type=jnp.float32
    ).astype(jnp.bfloat16)
    whole_frames = lax.all_gather(frame_part, "head", axis=1, tiled=True)
    frame_feat = lax.dynamic_index_in_dim(whole_frames, head_index // 2, 0, keepdims=False)
    patch_ids = jnp.arange(PPF, dtype=jnp.int32)
    tap_counts = jnp.sum(
        (patch_taps[:, :, None] == patch_ids[None, None, :]).astype(jnp.float32), axis=1
    )
    target = jnp.dot(
        tap_counts.astype(jnp.bfloat16), frame_feat, preferred_element_type=jnp.float32
    ) * (1.0 / TAPS)
    proj_float = projected.astype(jnp.float32)
    inner = jnp.sum(proj_float * target, axis=-1)
    proj_sq = jnp.sum(proj_float * proj_float, axis=-1) + 1e-06
    target_sq = jnp.sum(target * target, axis=-1) + 1e-06
    cosine = inner / jnp.sqrt(proj_sq * target_sq)
    return (hidden, projected, target, cosine)


CHUNK_HEADS = 2
MESH = pl.DeviceIdType.MESH


def fused_kernel(
    seq_count,
    q_ref,
    k_ref,
    v_ref,
    res_ref,
    w_ref,
    p1_ref,
    p2_ref,
    dino_ref,
    slot_ref,
    taps_ref,
    hid_out,
    proj_out,
    targ_out,
    cos_out,
    qkv,
    att,
    acc,
    w_v,
    p1_v,
    p2_v,
    res_v,
    hid_v,
    pre_v,
    lift_v,
    part_send,
    part_recv,
    dino_all,
    frame_sel,
    frame_buf,
    load_sem,
    own_sem,
    qkv_send,
    qkv_recv,
    att_send,
    att_recv,
    fwd_send,
    fwd_recv,
    part_ssem,
    part_rsem,
    dino_send,
    dino_recv,
    frame_send,
    frame_recv,
    hid_sem,
):
    seq = lax.axis_index("seq")
    me = lax.axis_index("head")
    chip = lax.div(me, 2)
    core = lax.rem(me, 2)
    sib = 2 * chip + (1 - core)
    cross = 2 * (1 - chip) + core
    diag = 2 * (1 - chip) + (1 - core)
    peers = (sib, cross, diag)
    rows = q_ref.shape[0]
    tokens = 4 * rows
    head_cols = q_ref.shape[1] // 4
    chunks = qkv.shape[1]
    width = qkv.shape[3]
    wide = w_v.shape[1]
    units = p1_v.shape[1]

    barrier = pltpu.get_barrier_semaphore()
    for peer in peers:
        pl.semaphore_signal(barrier, inc=1, device_id={"head": peer}, device_id_type=MESH)
    for step in range(1, seq_count):
        other = lax.rem(seq + step, seq_count)
        pl.semaphore_signal(barrier, inc=1, device_id={"seq": other}, device_id_type=MESH)
    pl.semaphore_wait(barrier, 3 + seq_count - 1)

    sources = (q_ref, k_ref, v_ref)
    my_rows = pl.ds(pl.multiple_of(me * rows, rows), rows)

    def columns(owner, i):
        return pl.ds(pl.multiple_of(owner * head_cols + i * width, width), width)

    qkv_copies = {}
    own_copies = {}

    def send_chunk(i):
        for t in range(3):
            for m in (2, 1, 0):
                copy = pltpu.make_async_remote_copy(
                    src_ref=sources[t].at[:, columns(peers[m], i)],
                    dst_ref=qkv.at[t, i, my_rows, :],
                    send_sem=qkv_send.at[t, m, i],
                    recv_sem=qkv_recv.at[t, m, i],
                    device_id={"head": peers[m]},
                    device_id_type=MESH,
                )
                copy.start()
                qkv_copies[t, m, i] = copy
            copy = pltpu.make_async_copy(
                sources[t].at[:, columns(me, i)], qkv.at[t, i, my_rows, :], own_sem.at[t, i]
            )
            copy.start()
            own_copies[t, i] = copy

    ahead = min(2, chunks)
    for i in range(ahead):
        send_chunk(i)

    dino_copies = []
    for step in range(1, seq_count):
        copy = pltpu.make_async_remote_copy(
            src_ref=dino_ref,
            dst_ref=dino_all.at[seq],
            send_sem=dino_send.at[step - 1],
            recv_sem=dino_recv.at[step - 1],
            device_id={"seq": lax.rem(seq + step, seq_count)},
            device_id_type=MESH,
        )
        copy.start()
        dino_copies.append(copy)
    loads = []
    for n, (src, dst) in enumerate(
        (
            (dino_ref, dino_all.at[seq]),
            (w_ref, w_v),
            (res_ref, res_v),
            (p1_ref, p1_v),
            (p2_ref, p2_v),
        )
    ):
        copy = pltpu.make_async_copy(src, dst, load_sem.at[n])
        copy.start()
        loads.append(copy)

    score_scale = HD ** (-0.5)
    block = min(256, tokens)
    blocks = tokens // block

    def attend_chunk(i):
        def body(n, carry):
            lanes = pl.ds(pl.multiple_of(lax.div(n, blocks) * HD, HD), HD)
            part = pl.ds(pl.multiple_of(lax.rem(n, blocks) * block, block), block)
            scores = lax.dot_general(
                qkv[0, i, part, lanes],
                qkv[1, i, :, lanes],
                (((1,), (1,)), ((), ())),
                preferred_element_type=jnp.float32,
            )
            scores = scores * score_scale
            top = jnp.max(scores, axis=-1, keepdims=True)
            exponents = jnp.exp(scores - top)
            total = jnp.sum(exponents, axis=-1, keepdims=True)
            mixed = jnp.dot(
                exponents.astype(jnp.bfloat16),
                qkv[2, i, :, lanes],
                preferred_element_type=jnp.float32,
            )
            att[me * chunks + i, part, lanes] = (mixed / total).astype(jnp.bfloat16)
            return carry

        lax.fori_loop(0, (width // HD) * blocks, body, 0)

    att_copies = {}

    def send_att(i):
        for m in (1, 0):
            copy = pltpu.make_async_remote_copy(
                src_ref=att.at[me * chunks + i],
                dst_ref=att.at[me * chunks + i],
                send_sem=att_send.at[m, i],
                recv_sem=att_recv.at[m, i],
                device_id={"head": peers[m]},
                device_id_type=MESH,
            )
            copy.start()
            att_copies[m, i] = copy

    fwd_copies = {}

    def forward(i):
        att_copies[1, i].wait_recv()
        copy = pltpu.make_async_remote_copy(
            src_ref=att.at[cross * chunks + i],
            dst_ref=att.at[cross * chunks + i],
            send_sem=fwd_send.at[i],
            recv_sem=fwd_recv.at[i],
            device_id={"head": sib},
            device_id_type=MESH,
        )
        copy.start()
        fwd_copies[i] = copy

    tile = 256

    def weight_rows(owner, i):
        return pl.ds(pl.multiple_of(owner * head_cols + i * width, width), width)

    def accumulate(pieces, first):
        def body(n, carry):
            cols = pl.ds(pl.multiple_of(n * tile, tile), tile)
            total = None if first else acc[:, cols]
            for owner, i in pieces:
                term = jnp.dot(
                    att[owner * chunks + i],
                    w_v[weight_rows(owner, i), cols],
                    preferred_element_type=jnp.float32,
                )
                total = term if total is None else total + term
            acc[:, cols] = total
            return carry

        lax.fori_loop(0, wide // tile, body, 0)

    frame_copies = []

    def pick_frames():
        for copy in dino_copies:
            copy.wait_recv()
        loads[0].wait()
        held = dino_ref.shape[0]
        for f in range(frame_sel.shape[0]):
            total = jnp.zeros(frame_sel.shape[1:], jnp.float32)
            for r in range(seq_count * held):
                hit = (slot_ref[r] == seq * held + f).astype(jnp.float32)
                total = total + hit * dino_all[r // held, r % held].astype(jnp.float32)
            frame_sel[f] = total.astype(jnp.bfloat16)
        for m, peer in enumerate(peers):
            copy = pltpu.make_async_remote_copy(
                src_ref=frame_sel.at[lax.div(peer, 2)],
                dst_ref=frame_buf.at[me],
                send_sem=frame_send.at[m],
                recv_sem=frame_recv.at[m],
                device_id={"head": peer},
                device_id_type=MESH,
            )
            copy.start()
            frame_copies.append(copy)
        frame_buf[me] = frame_sel[chip]

    def make_target():
        for copy in frame_copies:
            copy.wait_recv()
        patches = lax.broadcasted_iota(jnp.int32, (rows, PPF), 1)
        counts = jnp.zeros((rows, PPF), jnp.float32)
        for t in range(TAPS):
            counts = counts + (taps_ref[:, t : t + 1] == patches).astype(jnp.float32)
        frame = frame_buf[...].reshape(PPF, frame_buf.shape[2])
        targ_out[...] = jnp.dot(
            counts.astype(jnp.bfloat16), frame, preferred_element_type=jnp.float32
        ) * (1.0 / TAPS)

    last = chunks - 1
    for i in range(chunks):
        for t in range(3):
            for m in range(3):
                qkv_copies[t, m, i].wait_recv()
            own_copies[t, i].wait()
        if i + ahead < chunks:
            send_chunk(i + ahead)
        attend_chunk(i)
        send_att(i)
        if i == 1:
            loads[1].wait()
        if i >= 1:
            forward(i - 1)
            att_copies[0, i - 1].wait_recv()
            pieces = [(me, i - 1), (sib, i - 1), (cross, i - 1)]
            if i >= 2:
                fwd_copies[i - 2].wait_recv()
                pieces.append((diag, i - 2))
            accumulate(pieces, i == 1)
        if i == 2:
            pick_frames()
    att_copies[0, last].wait_recv()
    fwd_copies[last - 1].wait_recv()
    accumulate([(me, last), (sib, last), (diag, last - 1)], False)
    make_target()
    loads[2].wait()
    loads[3].wait()
    forward(last)
    fwd_copies[last].wait_recv()

    half = 2 * rows
    hid_copies = []

    def finish_hidden(which, slot):
        part = pl.ds(pl.multiple_of(which * half, half), half)

        def body(n, carry):
            cols = pl.ds(pl.multiple_of(n * tile, tile), tile)
            total = acc[part, cols]
            for owner in (cross, diag):
                total = total + jnp.dot(
                    att[owner * chunks + last, part, :],
                    w_v[weight_rows(owner, last), cols],
                    preferred_element_type=jnp.float32,
                )
            total = res_v[part, cols].astype(jnp.float32) + total
            hid_v[slot, :, cols] = total.astype(jnp.bfloat16)
            return carry

        lax.fori_loop(0, wide // tile, body, 0)
        copy = pltpu.make_async_copy(hid_v.at[slot], hid_out.at[part, :], hid_sem.at[slot])
        copy.start()
        hid_copies.append(copy)

    def partial_pre(slot):
        def body(n, carry):
            cols = pl.ds(pl.multiple_of(n * tile, tile), tile)
            pre_v[slot, :, cols] = jnp.dot(
                hid_v[slot], p1_v[:, cols], preferred_element_type=jnp.float32
            )
            return carry

        lax.fori_loop(0, units // tile, body, 0)

    def send_part(n, peer):
        copy = pltpu.make_async_remote_copy(
            src_ref=part_send.at[n],
            dst_ref=part_recv.at[n],
            send_sem=part_ssem.at[n],
            recv_sem=part_rsem.at[n],
            device_id={"head": peer},
            device_id_type=MESH,
        )
        copy.start()
        return copy

    mine = pl.ds(pl.multiple_of(core * rows, rows), rows)
    theirs = pl.ds(pl.multiple_of((1 - core) * rows, rows), rows)
    finish_hidden(1 - chip, 0)
    partial_pre(0)
    part_send[0] = pre_v[0, theirs, :].astype(jnp.bfloat16)
    first_part = send_part(0, sib)
    finish_hidden(chip, 1)
    first_part.wait_recv()
    part_send[1] = (pre_v[0, mine, :] + part_recv[0].astype(jnp.float32)).astype(jnp.bfloat16)
    second_part = send_part(1, cross)
    partial_pre(1)
    part_send[2] = pre_v[1, theirs, :].astype(jnp.bfloat16)
    third_part = send_part(2, sib)
    loads[4].wait()
    third_part.wait_recv()
    second_part.wait_recv()
    pre_act = (
        pre_v[1, mine, :] + part_recv[2].astype(jnp.float32) + part_recv[1].astype(jnp.float32)
    )
    lift_v[...] = (pre_act / (1.0 + jnp.exp(-pre_act))).astype(jnp.bfloat16)

    def project(n, sums):
        cols = pl.ds(pl.multiple_of(n * tile, tile), tile)
        value = jnp.dot(lift_v[...], p2_v[:, cols], preferred_element_type=jnp.float32).astype(
            jnp.bfloat16
        )
        proj_out[:, cols] = value
        value = value.astype(jnp.float32)
        target = targ_out[:, cols]
        inner, proj_sq, target_sq = sums
        return (
            inner + jnp.sum(value * target, axis=-1, keepdims=True),
            proj_sq + jnp.sum(value * value, axis=-1, keepdims=True),
            target_sq + jnp.sum(target * target, axis=-1, keepdims=True),
        )

    zero = jnp.zeros((rows, 1), jnp.float32)
    inner, proj_sq, target_sq = lax.fori_loop(
        0, p2_v.shape[1] // tile, project, (zero, zero, zero)
    )
    cos_out[...] = inner / jnp.sqrt((proj_sq + 1e-06) * (target_sq + 1e-06))

    for copy in hid_copies:
        copy.wait()
    for copy in qkv_copies.values():
        copy.wait_send()
    for copy in att_copies.values():
        copy.wait_send()
    for copy in fwd_copies.values():
        copy.wait_send()
    for copy in dino_copies + frame_copies + [first_part, second_part, third_part]:
        copy.wait_send()


def fused_device(
    query_rows,
    key_rows,
    value_rows,
    residual,
    out_weight,
    proj_first,
    proj_second,
    dino_feats,
    slot_frame,
    patch_taps,
):
    seq_count = lax.axis_size("seq")
    rows, all_cols = query_rows.shape
    tokens, wide = residual.shape
    units = proj_first.shape[1]
    feats = proj_second.shape[1]
    width = CHUNK_HEADS * HD
    chunks = all_cols // 4 // width
    held, part_patches = dino_feats.shape[:2]
    bf16 = jnp.bfloat16
    f32 = jnp.float32
    dma = pltpu.SemaphoreType.DMA
    any_spec = pl.BlockSpec(memory_space=pl.ANY)
    vmem_spec = pl.BlockSpec(memory_space=pltpu.VMEM)
    hidden, projected, target, cosine = pl.pallas_call(
        functools.partial(fused_kernel, seq_count),
        out_shape=(
            jax.ShapeDtypeStruct((tokens, wide), bf16),
            jax.ShapeDtypeStruct((rows, feats), bf16),
            jax.ShapeDtypeStruct((rows, feats), f32),
            jax.ShapeDtypeStruct((rows, 1), f32),
        ),
        in_specs=[any_spec] * 8 + [pl.BlockSpec(memory_space=pltpu.SMEM), vmem_spec],
        out_specs=(any_spec, vmem_spec, vmem_spec, vmem_spec),
        scratch_shapes=[
            pltpu.VMEM((3, chunks, tokens, width), bf16),
            pltpu.VMEM((4 * chunks, tokens, width), bf16),
            pltpu.VMEM((tokens, wide), f32),
            pltpu.VMEM(out_weight.shape, bf16),
            pltpu.VMEM(proj_first.shape, bf16),
            pltpu.VMEM(proj_second.shape, bf16),
            pltpu.VMEM((tokens, wide), bf16),
            pltpu.VMEM((2, 2 * rows, wide), bf16),
            pltpu.VMEM((2, 2 * rows, units), f32),
            pltpu.VMEM((rows, units), bf16),
            pltpu.VMEM((3, rows, units), bf16),
            pltpu.VMEM((3, rows, units), bf16),
            pltpu.VMEM((seq_count, held, part_patches, feats), bf16),
            pltpu.VMEM((held, part_patches, feats), bf16),
            pltpu.VMEM((4, part_patches, feats), bf16),
            dma((5,)),
            dma((3, chunks)),
            dma((3, 3, chunks)),
            dma((3, 3, chunks)),
            dma((2, chunks)),
            dma((2, chunks)),
            dma((chunks,)),
            dma((chunks,)),
            dma((3,)),
            dma((3,)),
            dma((seq_count - 1,)),
            dma((seq_count - 1,)),
            dma((3,)),
            dma((3,)),
            dma((2,)),
        ],
        compiler_params=pltpu.CompilerParams(
            collective_id=0, has_side_effects=True, vmem_limit_bytes=56 * 1024 * 1024
        ),
        cost_estimate=pl.CostEstimate(
            flops=2 * tokens * (all_cols * wide + wide * units),
            bytes_accessed=24 * 1024 * 1024,
            transcendentals=0,
        ),
        name="sublayer",
    )(
        query_rows,
        key_rows,
        value_rows,
        residual,
        out_weight,
        proj_first,
        proj_second,
        dino_feats,
        slot_frame,
        patch_taps,
    )
    return (hidden, projected, target, cosine.reshape(rows))


def solution(mesh):
    body = fused_device if mesh.shape["head"] == 4 else per_device
    return jax.shard_map(
        body,
        mesh=mesh,
        in_specs=(
            P(("seq", "head"), None),
            P(("seq", "head"), None),
            P(("seq", "head"), None),
            P("seq", "head"),
            P(None, "head"),
            P("head", None),
            P(),
            P("seq", "head", None),
            P(),
            P(("seq", "head"), None),
        ),
        out_specs=(
            P("seq", "head"),
            P(("seq", "head"), None),
            P(("seq", "head"), None),
            P(("seq", "head")),
        ),
        check_vma=False,
    )
```

```python
import functools

import jax
import jax.numpy as jnp
from jax import lax
from jax.experimental import pallas as pl
from jax.experimental.pallas import tpu as pltpu
from jax.sharding import PartitionSpec as P

HD = 128
PPF = 64
TAPS = 4
BLOCK = 512


def attend(operands):
    query_part, key_part, value_part = operands
    length = query_part.shape[0]
    item_count = query_part.shape[2]
    window_count = length // BLOCK
    score_scale = HD ** (-0.5)
    shaped = (
        query_part[:, 0].reshape(window_count, BLOCK, item_count, HD),
        key_part[:, 0].reshape(window_count, BLOCK, item_count, HD),
        value_part[:, 0].reshape(window_count, BLOCK, item_count, HD),
    )

    def one_window(parts):
        query_block, key_block, value_block = parts
        scores = (
            jnp.einsum("qhd,khd->hqk", query_block, key_block, preferred_element_type=jnp.float32)
            * score_scale
        )
        row_max = jnp.max(scores, axis=-1, keepdims=True)
        exponents = jnp.exp(scores - row_max)
        weights = (exponents / jnp.sum(exponents, axis=-1, keepdims=True)).astype(jnp.bfloat16)
        return jnp.einsum(
            "hqk,khd->qhd", weights, value_block, preferred_element_type=jnp.float32
        ).astype(jnp.bfloat16)

    return lax.map(one_window, shaped).reshape(length, 1, item_count, HD)


def per_device(
    query_rows,
    key_rows,
    value_rows,
    residual,
    out_weight,
    proj_first,
    proj_second,
    dino_feats,
    slot_frame,
    patch_taps,
):
    own_rows = query_rows.shape[0]
    group_count = lax.axis_size("head")
    per_group = query_rows.shape[1] // (HD * group_count)
    query_heads = query_rows.reshape(own_rows, group_count, per_group, HD)
    key_heads = key_rows.reshape(own_rows, group_count, per_group, HD)
    value_heads = value_rows.reshape(own_rows, group_count, per_group, HD)
    attended = attend(
        (
            lax.all_to_all(query_heads, "head", split_axis=1, concat_axis=0, tiled=True),
            lax.all_to_all(key_heads, "head", split_axis=1, concat_axis=0, tiled=True),
            lax.all_to_all(value_heads, "head", split_axis=1, concat_axis=0, tiled=True),
        )
    )
    seq_len = attended.shape[0]
    attended = attended.reshape(seq_len, per_group * HD)
    mixed_sum = jnp.dot(
        lax.all_gather(attended, "head", axis=1, tiled=True),
        out_weight,
        preferred_element_type=jnp.float32,
    )
    hidden = (residual.astype(jnp.float32) + mixed_sum).astype(jnp.bfloat16)
    pre_act = lax.psum_scatter(
        jnp.dot(hidden, proj_first, preferred_element_type=jnp.float32),
        "head",
        scatter_dimension=0,
        tiled=True,
    )
    lifted = jax.nn.silu(pre_act).astype(jnp.bfloat16)
    projected = jnp.dot(lifted, proj_second, preferred_element_type=jnp.float32).astype(
        jnp.bfloat16
    )
    seq_index = lax.axis_index("seq")
    head_index = lax.axis_index("head")
    frames_here = dino_feats.shape[0]
    wanted = seq_index * frames_here + jnp.arange(frames_here, dtype=jnp.int32)
    everything = lax.all_gather(dino_feats, "seq", axis=0, tiled=True)
    picker = (slot_frame[None, :] == wanted[:, None]).astype(jnp.bfloat16)
    frame_part = jnp.einsum(
        "ir,rpz->ipz", picker, everything, preferred_element_type=jnp.float32
    ).astype(jnp.bfloat16)
    whole_frames = lax.all_gather(frame_part, "head", axis=1, tiled=True)
    frame_feat = lax.dynamic_index_in_dim(whole_frames, head_index // 2, 0, keepdims=False)
    patch_ids = jnp.arange(PPF, dtype=jnp.int32)
    tap_counts = jnp.sum(
        (patch_taps[:, :, None] == patch_ids[None, None, :]).astype(jnp.float32), axis=1
    )
    target = jnp.dot(
        tap_counts.astype(jnp.bfloat16), frame_feat, preferred_element_type=jnp.float32
    ) * (1.0 / TAPS)
    proj_float = projected.astype(jnp.float32)
    inner = jnp.sum(proj_float * target, axis=-1)
    proj_sq = jnp.sum(proj_float * proj_float, axis=-1) + 1e-06
    target_sq = jnp.sum(target * target, axis=-1) + 1e-06
    cosine = inner / jnp.sqrt(proj_sq * target_sq)
    return (hidden, projected, target, cosine)


CHUNK_HEADS = 2
ROW_GROUPS = 4
MESH = pl.DeviceIdType.MESH


def fused_kernel(
    seq_count,
    q_ref,
    k_ref,
    v_ref,
    res_ref,
    w_ref,
    p1_ref,
    p2_ref,
    dino_ref,
    slot_ref,
    taps_ref,
    hid_out,
    proj_out,
    targ_out,
    cos_out,
    q_buf,
    kv_buf,
    att,
    acc,
    w_v,
    p1_v,
    p2_v,
    res_v,
    hid_v,
    pre_v,
    lift_v,
    sib_part,
    cross_send,
    cross_part,
    dino_all,
    frame_sel,
    frame_buf,
    load_sem,
    res_sem,
    own_sem,
    qkv_send,
    qkv_recv,
    sib_send,
    sib_recv,
    cross_ssem,
    cross_rsem,
    fwd_send,
    fwd_recv,
    part_send,
    part_recv,
    hop_send,
    hop_recv,
    dino_send,
    dino_recv,
    frame_send,
    frame_recv,
    hid_sem,
):
    seq = lax.axis_index("seq")
    me = lax.axis_index("head")
    chip = lax.div(me, 2)
    core = lax.rem(me, 2)
    sib = 2 * chip + (1 - core)
    cross = 2 * (1 - chip) + core
    diag = 2 * (1 - chip) + (1 - core)
    peers = (sib, cross, diag)
    groups, sub, all_cols = q_ref.shape
    rows = groups * sub
    tokens = 4 * rows
    group_rows = 4 * sub
    head_cols = all_cols // 4
    chunks = q_buf.shape[0]
    width = q_buf.shape[4]
    heads = width // HD
    wide = w_v.shape[1]
    units = p1_v.shape[1]
    tile = 256

    barrier = pltpu.get_barrier_semaphore()
    for peer in peers:
        pl.semaphore_signal(barrier, inc=1, device_id={"head": peer}, device_id_type=MESH)
    for step in range(1, seq_count):
        other = lax.rem(seq + step, seq_count)
        pl.semaphore_signal(barrier, inc=1, device_id={"seq": other}, device_id_type=MESH)
    pl.semaphore_wait(barrier, 3 + seq_count - 1)

    def send(src, dst, ssem, rsem, peer):
        copy = pltpu.make_async_remote_copy(
            src_ref=src,
            dst_ref=dst,
            send_sem=ssem,
            recv_sem=rsem,
            device_id={"head": peer},
            device_id_type=MESH,
        )
        copy.start()
        return copy

    my_rows = pl.ds(pl.multiple_of(me * rows, rows), rows)

    def columns(owner, i):
        return pl.ds(pl.multiple_of(owner * head_cols + i * width, width), width)

    def source(t, owner, i):
        if t == 0:
            return q_ref.at[:, :, columns(owner, i)]
        return (k_ref, v_ref)[t - 1].at[:, columns(owner, i)]

    def landing(t, i):
        if t == 0:
            return q_buf.at[i, :, me]
        return kv_buf.at[t - 1, i, my_rows, :]

    qkv_copies = {}
    own_copies = {}

    def send_chunk(i):
        for t in range(3):
            for m in (2, 1, 0):
                qkv_copies[t, m, i] = send(
                    source(t, peers[m], i),
                    landing(t, i),
                    qkv_send.at[t, m, i],
                    qkv_recv.at[t, m, i],
                    peers[m],
                )
            copy = pltpu.make_async_copy(source(t, me, i), landing(t, i), own_sem.at[t, i])
            copy.start()
            own_copies[t, i] = copy

    ahead = min(2, chunks)
    for i in range(ahead):
        send_chunk(i)

    dino_copies = []
    for step in range(1, seq_count):
        copy = pltpu.make_async_remote_copy(
            src_ref=dino_ref,
            dst_ref=dino_all.at[seq],
            send_sem=dino_send.at[step - 1],
            recv_sem=dino_recv.at[step - 1],
            device_id={"seq": lax.rem(seq + step, seq_count)},
            device_id_type=MESH,
        )
        copy.start()
        dino_copies.append(copy)
    loads = []
    for n, (src, dst) in enumerate(
        ((dino_ref, dino_all.at[seq]), (w_ref, w_v), (p1_ref, p1_v), (p2_ref, p2_v))
    ):
        copy = pltpu.make_async_copy(src, dst, load_sem.at[n])
        copy.start()
        loads.append(copy)
    res_loads = []
    for g in range(groups):
        copy = pltpu.make_async_copy(res_ref.at[:, g], res_v.at[g], res_sem.at[g])
        copy.start()
        res_loads.append(copy)

    score_scale = HD ** (-0.5)

    def attend(i, n, first, count):
        lanes = pl.ds(pl.multiple_of(n * HD, HD), HD)
        query = q_buf[i, pl.ds(first, count), :, :, lanes].reshape(count * group_rows, HD)
        scores = lax.dot_general(
            query,
            kv_buf[0, i, :, lanes],
            (((1,), (1,)), ((), ())),
            preferred_element_type=jnp.float32,
        )
        scores = scores * score_scale
        top = jnp.max(scores, axis=-1, keepdims=True)
        exponents = jnp.exp(scores - top)
        total = jnp.sum(exponents, axis=-1, keepdims=True)
        mixed = jnp.dot(
            exponents.astype(jnp.bfloat16),
            kv_buf[1, i, :, lanes],
            preferred_element_type=jnp.float32,
        )
        mixed = (mixed / total).astype(jnp.bfloat16)
        place = pl.ds(pl.multiple_of(me * head_cols + i * width + n * HD, HD), HD)
        att[pl.ds(first, count), :, place] = mixed.reshape(count, group_rows, HD)

    both = min(2, groups)

    def attend_chunk(i):
        def body(n, carry):
            attend(i, lax.div(n, groups // both), lax.rem(n, groups // both) * both, both)
            return carry

        lax.fori_loop(0, heads * (groups // both), body, 0)

    last = chunks - 1
    early = last * width

    def owned(g, owner, start, size):
        return att.at[g, :, pl.ds(pl.multiple_of(owner * head_cols + start, width), size)]

    att_copies = {}

    def send_att(g, part):
        mine = owned(g, me, 0, early) if part == 0 else owned(g, me, early, width)
        att_copies[1, g, part] = send(
            mine, mine, cross_ssem.at[g, part], cross_rsem.at[g, part], cross
        )
        att_copies[0, g, part] = send(mine, mine, sib_send.at[g, part], sib_recv.at[g, part], sib)

    frame_copies = []

    def pick_frames():
        for copy in dino_copies:
            copy.wait_recv()
        loads[0].wait()
        held = dino_ref.shape[0]
        for f in range(frame_sel.shape[0]):
            total = jnp.zeros(frame_sel.shape[1:], jnp.float32)
            for r in range(seq_count * held):
                hit = (slot_ref[r] == seq * held + f).astype(jnp.float32)
                total = total + hit * dino_all[r // held, r % held].astype(jnp.float32)
            frame_sel[f] = total.astype(jnp.bfloat16)
        for m, (peer, which) in enumerate(((sib, chip), (cross, 1 - chip))):
            frame_copies.append(
                send(
                    frame_sel.at[which],
                    frame_buf.at[me],
                    frame_send.at[m],
                    frame_recv.at[m],
                    peer,
                )
            )
        frame_buf[me] = frame_sel[chip]

    def forward_frames():
        frame_copies[1].wait_recv()
        frame_copies.append(
            send(
                frame_buf.at[cross], frame_buf.at[cross], frame_send.at[2], frame_recv.at[2], sib
            )
        )

    def make_target():
        frame_copies[0].wait_recv()
        frame_copies[2].wait_recv()
        patches = lax.broadcasted_iota(jnp.int32, (PPF, rows), 0)
        counts = jnp.zeros((PPF, rows), jnp.float32)
        for t in range(TAPS):
            counts = counts + (taps_ref[t : t + 1, :] == patches).astype(jnp.float32)
        counts = counts.T.astype(jnp.bfloat16)
        frame = frame_buf[...].reshape(PPF, frame_buf.shape[2])
        targ_out[...] = jnp.dot(counts, frame, preferred_element_type=jnp.float32) * (1.0 / TAPS)

    for i in range(last):
        for t in range(3):
            for m in range(3):
                qkv_copies[t, m, i].wait_recv()
            own_copies[t, i].wait()
        if i + ahead < chunks:
            send_chunk(i + ahead)
        attend_chunk(i)
    send_att(0, 0)
    pick_frames()
    for t in range(3):
        for m in range(3):
            qkv_copies[t, m, last].wait_recv()
        own_copies[t, last].wait()
    for g in range(groups):

        def last_heads(n, carry, g=g):
            attend(last, n, g, 1)
            return carry

        lax.fori_loop(0, heads, last_heads, 0)
        send_att(g, 1)
        if g + 1 < groups:
            send_att(g + 1, 0)
    forward_frames()
    loads[1].wait()

    def products(g, owners, cols):
        total = None
        for owner in owners:
            part = pl.ds(pl.multiple_of(owner * head_cols, head_cols), head_cols)
            term = jnp.dot(
                att[g, :, part], w_v[part, cols], preferred_element_type=jnp.float32
            )
            total = term if total is None else total + term
        return total

    def over_tiles(count, step):
        def body(n, carry):
            step(pl.ds(pl.multiple_of(n * tile, tile), tile))
            return carry

        lax.fori_loop(0, count // tile, body, 0)

    hid_copies = []
    part_copies = {}
    hop_copies = {}
    fwd_copies = {}

    def reduce_hop(g):
        part_copies[g, 0].wait_recv()
        cross_send[g] = (pre_v[g, cross] + sib_part[g, 0]).astype(jnp.bfloat16)
        hop_copies[g] = send(
            cross_send.at[g], cross_part.at[g], hop_send.at[g], hop_recv.at[g], cross
        )

    for g in range(groups):
        for part in range(2):
            att_copies[0, g, part].wait_recv()

        def near(cols, g=g):
            acc[:, cols] = products(g, (me, sib), cols)

        over_tiles(wide, near)
        if g >= 1:
            reduce_hop(g - 1)
        if g == groups - 1:
            make_target()
        for part in range(2):
            att_copies[1, g, part].wait_recv()
        theirs = owned(g, cross, 0, head_cols)
        fwd_copies[g] = send(theirs, theirs, fwd_send.at[g], fwd_recv.at[g], sib)

        def far(cols, g=g):
            acc[:, cols] = acc[:, cols] + products(g, (cross,), cols)

        over_tiles(wide, far)
        fwd_copies[g].wait_recv()
        res_loads[g].wait()

        def close(cols, g=g):
            total = acc[:, cols] + products(g, (diag,), cols)
            total = total.reshape(4, sub, tile) + res_v[g, :, :, cols].astype(jnp.float32)
            hid_v[g, :, :, cols] = total.astype(jnp.bfloat16)

        over_tiles(wide, close)
        copy = pltpu.make_async_copy(hid_v.at[g], hid_out.at[:, g], hid_sem.at[g])
        copy.start()
        hid_copies.append(copy)
        if g == 0:
            loads[2].wait()

        def first_layer(cols, g=g):
            value = jnp.dot(
                hid_v[g].reshape(group_rows, wide), p1_v[:, cols],
                preferred_element_type=jnp.float32,
            )
            pre_v[g, :, :, cols] = value.reshape(4, sub, tile)

        over_tiles(units, first_layer)
        for n, owner in enumerate((diag, sib)):
            part_copies[g, n] = send(
                pre_v.at[g, owner],
                sib_part.at[g, n],
                part_send.at[g, n],
                part_recv.at[g, n],
                sib,
            )
    reduce_hop(groups - 1)
    loads[3].wait()
    for g in range(groups):
        part_copies[g, 1].wait_recv()
        hop_copies[g].wait_recv()
        pre_act = pre_v[g, me] + sib_part[g, 1] + cross_part[g].astype(jnp.float32)
        lift_v[pl.ds(g * sub, sub), :] = (pre_act / (1.0 + jnp.exp(-pre_act))).astype(
            jnp.bfloat16
        )

    def project(n, sums):
        cols = pl.ds(pl.multiple_of(n * tile, tile), tile)
        value = jnp.dot(lift_v[...], p2_v[:, cols], preferred_element_type=jnp.float32).astype(
            jnp.bfloat16
        )
        proj_out[:, cols] = value
        value = value.astype(jnp.float32)
        target = targ_out[:, cols]
        inner, proj_sq, target_sq = sums
        return (
            inner + jnp.sum(value * target, axis=-1, keepdims=True),
            proj_sq + jnp.sum(value * value, axis=-1, keepdims=True),
            target_sq + jnp.sum(target * target, axis=-1, keepdims=True),
        )

    zero = jnp.zeros((rows, 1), jnp.float32)
    inner, proj_sq, target_sq = lax.fori_loop(
        0, p2_v.shape[1] // tile, project, (zero, zero, zero)
    )
    cosine = inner / jnp.sqrt((proj_sq + 1e-06) * (target_sq + 1e-06))
    cos_out[...] = jnp.broadcast_to(cosine, (rows, rows)).T[0:1, :]

    for copy in hid_copies:
        copy.wait()
    for copies in (qkv_copies, att_copies, fwd_copies, part_copies, hop_copies):
        for copy in copies.values():
            copy.wait_send()
    for copy in dino_copies + frame_copies:
        copy.wait_send()


def fused_device(
    query_rows,
    key_rows,
    value_rows,
    residual,
    out_weight,
    proj_first,
    proj_second,
    dino_feats,
    slot_frame,
    patch_taps,
):
    seq_count = lax.axis_size("seq")
    rows, all_cols = query_rows.shape
    tokens, wide = residual.shape
    units = proj_first.shape[1]
    feats = proj_second.shape[1]
    width = CHUNK_HEADS * HD
    chunks = all_cols // 4 // width
    groups = ROW_GROUPS
    sub = rows // groups
    held, part_patches = dino_feats.shape[:2]
    bf16 = jnp.bfloat16
    f32 = jnp.float32
    dma = pltpu.SemaphoreType.DMA
    any_spec = pl.BlockSpec(memory_space=pl.ANY)
    vmem_spec = pl.BlockSpec(memory_space=pltpu.VMEM)
    hidden, projected, target, cosine = pl.pallas_call(
        functools.partial(fused_kernel, seq_count),
        out_shape=(
            jax.ShapeDtypeStruct((4, groups, sub, wide), bf16),
            jax.ShapeDtypeStruct((rows, feats), bf16),
            jax.ShapeDtypeStruct((rows, feats), f32),
            jax.ShapeDtypeStruct((1, rows), f32),
        ),
        in_specs=[any_spec] * 8 + [pl.BlockSpec(memory_space=pltpu.SMEM), vmem_spec],
        out_specs=(any_spec, vmem_spec, vmem_spec, vmem_spec),
        scratch_shapes=[
            pltpu.VMEM((chunks, groups, 4, sub, width), bf16),
            pltpu.VMEM((2, chunks, tokens, width), bf16),
            pltpu.VMEM((groups, 4 * sub, all_cols), bf16),
            pltpu.VMEM((4 * sub, wide), f32),
            pltpu.VMEM(out_weight.shape, bf16),
            pltpu.VMEM(proj_first.shape, bf16),
            pltpu.VMEM(proj_second.shape, bf16),
            pltpu.VMEM((groups, 4, sub, wide), bf16),
            pltpu.VMEM((groups, 4, sub, wide), bf16),
            pltpu.VMEM((groups, 4, sub, units), f32),
            pltpu.VMEM((rows, units), bf16),
            pltpu.VMEM((groups, 2, sub, units), f32),
            pltpu.VMEM((groups, sub, units), bf16),
            pltpu.VMEM((groups, sub, units), bf16),
            pltpu.VMEM((seq_count, held, part_patches, feats), bf16),
            pltpu.VMEM((held, part_patches, feats), bf16),
            pltpu.VMEM((4, part_patches, feats), bf16),
            dma((4,)),
            dma((groups,)),
            dma((3, chunks)),
            dma((3, 3, chunks)),
            dma((3, 3, chunks)),
            dma((groups, 2)),
            dma((groups, 2)),
            dma((groups, 2)),
            dma((groups, 2)),
            dma((groups,)),
            dma((groups,)),
            dma((groups, 2)),
            dma((groups, 2)),
            dma((groups,)),
            dma((groups,)),
            dma((seq_count - 1,)),
            dma((seq_count - 1,)),
            dma((3,)),
            dma((3,)),
            dma((groups,)),
        ],
        compiler_params=pltpu.CompilerParams(
            collective_id=0, has_side_effects=True, vmem_limit_bytes=56 * 1024 * 1024
        ),
        cost_estimate=pl.CostEstimate(
            flops=2 * tokens * (all_cols * wide + wide * units),
            bytes_accessed=24 * 1024 * 1024,
            transcendentals=0,
        ),
        name="sublayer",
    )(
        query_rows.reshape(groups, sub, all_cols),
        key_rows,
        value_rows,
        residual.reshape(4, groups, sub, wide),
        out_weight,
        proj_first,
        proj_second,
        dino_feats,
        slot_frame,
        patch_taps.T,
    )
    return (hidden.reshape(tokens, wide), projected, target, cosine.reshape(rows))


def solution(mesh):
    body = fused_device if mesh.shape["head"] == 4 else per_device
    return jax.shard_map(
        body,
        mesh=mesh,
        in_specs=(
            P(("seq", "head"), None),
            P(("seq", "head"), None),
            P(("seq", "head"), None),
            P("seq", "head"),
            P(None, "head"),
            P("head", None),
            P(),
            P("seq", "head", None),
            P(),
            P(("seq", "head"), None),
        ),
        out_specs=(
            P("seq", "head"),
            P(("seq", "head"), None),
            P(("seq", "head"), None),
            P(("seq", "head")),
        ),
        check_vma=False,
    )
```

```python
import functools

import jax
import jax.numpy as jnp
from jax import lax
from jax.experimental import pallas as pl
from jax.experimental.pallas import tpu as pltpu
from jax.sharding import PartitionSpec as P

HD = 128
PPF = 64
TAPS = 4
BLOCK = 512


def attend(operands):
    query_part, key_part, value_part = operands
    length = query_part.shape[0]
    item_count = query_part.shape[2]
    window_count = length // BLOCK
    score_scale = HD ** (-0.5)
    shaped = (
        query_part[:, 0].reshape(window_count, BLOCK, item_count, HD),
        key_part[:, 0].reshape(window_count, BLOCK, item_count, HD),
        value_part[:, 0].reshape(window_count, BLOCK, item_count, HD),
    )

    def one_window(parts):
        query_block, key_block, value_block = parts
        scores = (
            jnp.einsum("qhd,khd->hqk", query_block, key_block, preferred_element_type=jnp.float32)
            * score_scale
        )
        row_max = jnp.max(scores, axis=-1, keepdims=True)
        exponents = jnp.exp(scores - row_max)
        weights = (exponents / jnp.sum(exponents, axis=-1, keepdims=True)).astype(jnp.bfloat16)
        return jnp.einsum(
            "hqk,khd->qhd", weights, value_block, preferred_element_type=jnp.float32
        ).astype(jnp.bfloat16)

    return lax.map(one_window, shaped).reshape(length, 1, item_count, HD)


def per_device(
    query_rows,
    key_rows,
    value_rows,
    residual,
    out_weight,
    proj_first,
    proj_second,
    dino_feats,
    slot_frame,
    patch_taps,
):
    own_rows = query_rows.shape[0]
    group_count = lax.axis_size("head")
    per_group = query_rows.shape[1] // (HD * group_count)
    query_heads = query_rows.reshape(own_rows, group_count, per_group, HD)
    key_heads = key_rows.reshape(own_rows, group_count, per_group, HD)
    value_heads = value_rows.reshape(own_rows, group_count, per_group, HD)
    attended = attend(
        (
            lax.all_to_all(query_heads, "head", split_axis=1, concat_axis=0, tiled=True),
            lax.all_to_all(key_heads, "head", split_axis=1, concat_axis=0, tiled=True),
            lax.all_to_all(value_heads, "head", split_axis=1, concat_axis=0, tiled=True),
        )
    )
    seq_len = attended.shape[0]
    attended = attended.reshape(seq_len, per_group * HD)
    mixed_sum = jnp.dot(
        lax.all_gather(attended, "head", axis=1, tiled=True),
        out_weight,
        preferred_element_type=jnp.float32,
    )
    hidden = (residual.astype(jnp.float32) + mixed_sum).astype(jnp.bfloat16)
    pre_act = lax.psum_scatter(
        jnp.dot(hidden, proj_first, preferred_element_type=jnp.float32),
        "head",
        scatter_dimension=0,
        tiled=True,
    )
    lifted = jax.nn.silu(pre_act).astype(jnp.bfloat16)
    projected = jnp.dot(lifted, proj_second, preferred_element_type=jnp.float32).astype(
        jnp.bfloat16
    )
    seq_index = lax.axis_index("seq")
    head_index = lax.axis_index("head")
    frames_here = dino_feats.shape[0]
    wanted = seq_index * frames_here + jnp.arange(frames_here, dtype=jnp.int32)
    everything = lax.all_gather(dino_feats, "seq", axis=0, tiled=True)
    picker = (slot_frame[None, :] == wanted[:, None]).astype(jnp.bfloat16)
    frame_part = jnp.einsum(
        "ir,rpz->ipz", picker, everything, preferred_element_type=jnp.float32
    ).astype(jnp.bfloat16)
    whole_frames = lax.all_gather(frame_part, "head", axis=1, tiled=True)
    frame_feat = lax.dynamic_index_in_dim(whole_frames, head_index // 2, 0, keepdims=False)
    patch_ids = jnp.arange(PPF, dtype=jnp.int32)
    tap_counts = jnp.sum(
        (patch_taps[:, :, None] == patch_ids[None, None, :]).astype(jnp.float32), axis=1
    )
    target = jnp.dot(
        tap_counts.astype(jnp.bfloat16), frame_feat, preferred_element_type=jnp.float32
    ) * (1.0 / TAPS)
    proj_float = projected.astype(jnp.float32)
    inner = jnp.sum(proj_float * target, axis=-1)
    proj_sq = jnp.sum(proj_float * proj_float, axis=-1) + 1e-06
    target_sq = jnp.sum(target * target, axis=-1) + 1e-06
    cosine = inner / jnp.sqrt(proj_sq * target_sq)
    return (hidden, projected, target, cosine)


CHUNK_HEADS = 2
ROW_GROUPS = 4
MESH = pl.DeviceIdType.MESH


def fused_kernel(
    seq_count,
    q_ref,
    k_ref,
    v_ref,
    res_ref,
    w_ref,
    p1_ref,
    dino_ref,
    slot_ref,
    hid_out,
    lift_out,
    frame_out,
    q_buf,
    kv_buf,
    att,
    acc,
    w_v,
    p1_v,
    res_v,
    hid_v,
    pre_v,
    sib_part,
    cross_send,
    cross_part,
    dino_all,
    frame_sel,
    frame_buf,
    load_sem,
    res_sem,
    own_sem,
    qkv_send,
    qkv_recv,
    sib_send,
    sib_recv,
    cross_ssem,
    cross_rsem,
    fwd_send,
    fwd_recv,
    part_send,
    part_recv,
    hop_send,
    hop_recv,
    dino_send,
    dino_recv,
    frame_send,
    frame_recv,
    hid_sem,
):
    seq = lax.axis_index("seq")
    me = lax.axis_index("head")
    chip = lax.div(me, 2)
    core = lax.rem(me, 2)
    sib = 2 * chip + (1 - core)
    cross = 2 * (1 - chip) + core
    diag = 2 * (1 - chip) + (1 - core)
    peers = (sib, cross, diag)
    groups, sub, all_cols = q_ref.shape
    rows = groups * sub
    tokens = 4 * rows
    group_rows = 4 * sub
    head_cols = all_cols // 4
    chunks = q_buf.shape[0]
    width = q_buf.shape[4]
    heads = width // HD
    wide = w_v.shape[1]
    units = p1_v.shape[1]
    tile = 256

    barrier = pltpu.get_barrier_semaphore()
    for peer in peers:
        pl.semaphore_signal(barrier, inc=1, device_id={"head": peer}, device_id_type=MESH)
    for step in range(1, seq_count):
        other = lax.rem(seq + step, seq_count)
        pl.semaphore_signal(barrier, inc=1, device_id={"seq": other}, device_id_type=MESH)
    pl.semaphore_wait(barrier, 3 + seq_count - 1)

    def send(src, dst, ssem, rsem, peer):
        copy = pltpu.make_async_remote_copy(
            src_ref=src,
            dst_ref=dst,
            send_sem=ssem,
            recv_sem=rsem,
            device_id={"head": peer},
            device_id_type=MESH,
        )
        copy.start()
        return copy

    my_rows = pl.ds(pl.multiple_of(me * rows, rows), rows)

    def columns(owner, i):
        return pl.ds(pl.multiple_of(owner * head_cols + i * width, width), width)

    def source(t, owner, i):
        if t == 0:
            return q_ref.at[:, :, columns(owner, i)]
        return (k_ref, v_ref)[t - 1].at[:, columns(owner, i)]

    def landing(t, i):
        if t == 0:
            return q_buf.at[i, :, me]
        return kv_buf.at[t - 1, i, my_rows, :]

    qkv_copies = {}
    own_copies = {}

    def send_chunk(i):
        for t in range(3):
            for m in (2, 1, 0):
                qkv_copies[t, m, i] = send(
                    source(t, peers[m], i),
                    landing(t, i),
                    qkv_send.at[t, m, i],
                    qkv_recv.at[t, m, i],
                    peers[m],
                )
            copy = pltpu.make_async_copy(source(t, me, i), landing(t, i), own_sem.at[t, i])
            copy.start()
            own_copies[t, i] = copy

    ahead = min(2, chunks)
    for i in range(ahead):
        send_chunk(i)

    dino_copies = []
    for step in range(1, seq_count):
        copy = pltpu.make_async_remote_copy(
            src_ref=dino_ref,
            dst_ref=dino_all.at[seq],
            send_sem=dino_send.at[step - 1],
            recv_sem=dino_recv.at[step - 1],
            device_id={"seq": lax.rem(seq + step, seq_count)},
            device_id_type=MESH,
        )
        copy.start()
        dino_copies.append(copy)
    loads = []
    for n, (src, dst) in enumerate(
        ((dino_ref, dino_all.at[seq]), (w_ref, w_v), (p1_ref, p1_v))
    ):
        copy = pltpu.make_async_copy(src, dst, load_sem.at[n])
        copy.start()
        loads.append(copy)
    res_loads = []
    for g in range(groups):
        copy = pltpu.make_async_copy(res_ref.at[:, g], res_v.at[g], res_sem.at[g])
        copy.start()
        res_loads.append(copy)

    score_scale = HD ** (-0.5)

    def attend(i, n, first, count):
        lanes = pl.ds(pl.multiple_of(n * HD, HD), HD)
        query = q_buf[i, pl.ds(first, count), :, :, lanes].reshape(count * group_rows, HD)
        scores = lax.dot_general(
            query,
            kv_buf[0, i, :, lanes],
            (((1,), (1,)), ((), ())),
            preferred_element_type=jnp.float32,
        )
        scores = scores * score_scale
        top = jnp.max(scores, axis=-1, keepdims=True)
        exponents = jnp.exp(scores - top)
        total = jnp.sum(exponents, axis=-1, keepdims=True)
        mixed = jnp.dot(
            exponents.astype(jnp.bfloat16),
            kv_buf[1, i, :, lanes],
            preferred_element_type=jnp.float32,
        )
        mixed = (mixed / total).astype(jnp.bfloat16)
        place = pl.ds(pl.multiple_of(me * head_cols + i * width + n * HD, HD), HD)
        att[pl.ds(first, count), :, place] = mixed.reshape(count, group_rows, HD)

    both = min(2, groups)

    def attend_chunk(i):
        def body(n, carry):
            attend(i, lax.div(n, groups // both), lax.rem(n, groups // both) * both, both)
            return carry

        lax.fori_loop(0, heads * (groups // both), body, 0)

    last = chunks - 1
    early = last * width

    def owned(g, owner, start, size):
        return att.at[g, :, pl.ds(pl.multiple_of(owner * head_cols + start, width), size)]

    att_copies = {}

    def send_att(g, part):
        if part == 0:
            mine = owned(g, me, 0, early)
        elif g == 0:
            mine = owned(g, me, early, width)
        else:
            mine = owned(g, me, 0, head_cols)
        att_copies[1, g, part] = send(
            mine, mine, cross_ssem.at[g, part], cross_rsem.at[g, part], cross
        )
        att_copies[0, g, part] = send(mine, mine, sib_send.at[g, part], sib_recv.at[g, part], sib)

    frame_copies = []

    def pick_frames():
        for copy in dino_copies:
            copy.wait_recv()
        loads[0].wait()
        held = dino_ref.shape[0]
        for f in range(frame_sel.shape[0]):
            total = jnp.zeros(frame_sel.shape[1:], jnp.float32)
            for r in range(seq_count * held):
                hit = (slot_ref[r] == seq * held + f).astype(jnp.float32)
                total = total + hit * dino_all[r // held, r % held].astype(jnp.float32)
            frame_sel[f] = total.astype(jnp.bfloat16)
        for m, (peer, which) in enumerate(((sib, chip), (cross, 1 - chip))):
            frame_copies.append(
                send(
                    frame_sel.at[which],
                    frame_buf.at[me],
                    frame_send.at[m],
                    frame_recv.at[m],
                    peer,
                )
            )
        frame_buf[me] = frame_sel[chip]

    def forward_frames():
        frame_copies[1].wait_recv()
        frame_copies.append(
            send(
                frame_buf.at[cross], frame_buf.at[cross], frame_send.at[2], frame_recv.at[2], sib
            )
        )

    def place_frames():
        frame_copies[0].wait_recv()
        frame_copies[2].wait_recv()
        frame_out[...] = frame_buf[...].reshape(frame_out.shape)

    for i in range(last):
        for t in range(3):
            for m in range(3):
                qkv_copies[t, m, i].wait_recv()
            own_copies[t, i].wait()
        if i + ahead < chunks:
            send_chunk(i + ahead)
        attend_chunk(i)
    send_att(0, 0)
    for t in range(3):
        for m in range(3):
            qkv_copies[t, m, last].wait_recv()
        own_copies[t, last].wait()
    for g in range(groups):

        def last_heads(n, carry, g=g):
            attend(last, n, g, 1)
            return carry

        lax.fori_loop(0, heads, last_heads, 0)
        send_att(g, 1)
    pick_frames()
    loads[1].wait()

    def products(g, owners, cols):
        total = None
        for owner in owners:
            part = pl.ds(pl.multiple_of(owner * head_cols, head_cols), head_cols)
            term = jnp.dot(
                att[g, :, part], w_v[part, cols], preferred_element_type=jnp.float32
            )
            total = term if total is None else total + term
        return total

    def over_tiles(count, step):
        def body(n, carry):
            step(pl.ds(pl.multiple_of(n * tile, tile), tile))
            return carry

        lax.fori_loop(0, count // tile, body, 0)

    hid_copies = []
    part_copies = {}
    hop_copies = {}
    fwd_copies = {}

    def reduce_hop(g):
        part_copies[g, 0].wait_recv()
        cross_send[g] = (pre_v[g, cross] + sib_part[g, 0]).astype(jnp.bfloat16)
        hop_copies[g] = send(
            cross_send.at[g], cross_part.at[g], hop_send.at[g], hop_recv.at[g], cross
        )

    for g in range(groups):
        for part in (0, 1) if g == 0 else (1,):
            att_copies[0, g, part].wait_recv()

        def near(cols, g=g):
            acc[:, cols] = products(g, (me, sib), cols)

        over_tiles(wide, near)
        if g >= 1:
            reduce_hop(g - 1)
        for part in (0, 1) if g == 0 else (1,):
            att_copies[1, g, part].wait_recv()
        theirs = owned(g, cross, 0, head_cols)
        fwd_copies[g] = send(theirs, theirs, fwd_send.at[g], fwd_recv.at[g], sib)

        def far(cols, g=g):
            acc[:, cols] = acc[:, cols] + products(g, (cross,), cols)

        over_tiles(wide, far)
        fwd_copies[g].wait_recv()
        res_loads[g].wait()

        def close(cols, g=g):
            total = acc[:, cols] + products(g, (diag,), cols)
            total = total.reshape(4, sub, tile) + res_v[g, :, :, cols].astype(jnp.float32)
            hid_v[g, :, :, cols] = total.astype(jnp.bfloat16)

        over_tiles(wide, close)
        copy = pltpu.make_async_copy(hid_v.at[g], hid_out.at[:, g], hid_sem.at[g])
        copy.start()
        hid_copies.append(copy)
        if g == 0:
            loads[2].wait()

        def first_layer(cols, g=g):
            value = jnp.dot(
                hid_v[g].reshape(group_rows, wide), p1_v[:, cols],
                preferred_element_type=jnp.float32,
            )
            pre_v[g, :, :, cols] = value.reshape(4, sub, tile)

        over_tiles(units, first_layer)
        for n, owner in enumerate((diag, sib)):
            part_copies[g, n] = send(
                pre_v.at[g, owner],
                sib_part.at[g, n],
                part_send.at[g, n],
                part_recv.at[g, n],
                sib,
            )
    forward_frames()
    reduce_hop(groups - 1)
    place_frames()
    for g in range(groups):
        part_copies[g, 1].wait_recv()
        hop_copies[g].wait_recv()
        pre_act = pre_v[g, me] + sib_part[g, 1] + cross_part[g].astype(jnp.float32)
        lift_out[pl.ds(g * sub, sub), :] = (pre_act / (1.0 + jnp.exp(-pre_act))).astype(
            jnp.bfloat16
        )

    for copy in hid_copies:
        copy.wait()
    for copies in (qkv_copies, att_copies, fwd_copies, part_copies, hop_copies):
        for copy in copies.values():
            copy.wait_send()
    for copy in dino_copies + frame_copies:
        copy.wait_send()


def project_kernel(
    hid_ref,
    lift_ref,
    frame_ref,
    taps_ref,
    p2_ref,
    hid_out,
    proj_out,
    targ_out,
    cos_out,
    hid_v,
    p2_v,
    proj_v,
    targ_v,
    hid_in_sem,
    hid_out_sem,
    p2_sem,
    out_sem,
):
    rows = lift_ref.shape[0]
    tile = 256
    tiles = p2_v.shape[1] // tile
    parts = hid_v.shape[0]
    p2_loads = []
    for n in range(tiles):
        cols = pl.ds(n * tile, tile)
        copy = pltpu.make_async_copy(p2_ref.at[:, cols], p2_v.at[:, cols], p2_sem.at[n])
        copy.start()
        p2_loads.append(copy)
    hid_loads = []
    for n in range(parts):
        copy = pltpu.make_async_copy(hid_ref.at[n], hid_v.at[n], hid_in_sem.at[n])
        copy.start()
        hid_loads.append(copy)
    patches = lax.broadcasted_iota(jnp.int32, (PPF, rows), 0)
    counts = jnp.zeros((PPF, rows), jnp.float32)
    for t in range(TAPS):
        counts = counts + (taps_ref[t : t + 1, :] == patches).astype(jnp.float32)
    counts = counts.T.astype(jnp.bfloat16)
    targ_v[...] = jnp.dot(counts, frame_ref[...], preferred_element_type=jnp.float32) * (
        1.0 / TAPS
    )
    stores = [pltpu.make_async_copy(targ_v, targ_out, out_sem.at[0])]
    stores[0].start()
    inner = jnp.zeros((rows, 1), jnp.float32)
    proj_sq = jnp.zeros((rows, 1), jnp.float32)
    target_sq = jnp.zeros((rows, 1), jnp.float32)
    for n in range(tiles):
        cols = pl.ds(n * tile, tile)
        p2_loads[n].wait()
        value = jnp.dot(
            lift_ref[...], p2_v[:, cols], preferred_element_type=jnp.float32
        ).astype(jnp.bfloat16)
        proj_v[:, cols] = value
        value = value.astype(jnp.float32)
        target = targ_v[:, cols]
        inner = inner + jnp.sum(value * target, axis=-1, keepdims=True)
        proj_sq = proj_sq + jnp.sum(value * value, axis=-1, keepdims=True)
        target_sq = target_sq + jnp.sum(target * target, axis=-1, keepdims=True)
        if n == 0:
            for m in range(parts):
                hid_loads[m].wait()
                copy = pltpu.make_async_copy(hid_v.at[m], hid_out.at[m], hid_out_sem.at[m])
                copy.start()
                stores.append(copy)
    copy = pltpu.make_async_copy(proj_v, proj_out, out_sem.at[1])
    copy.start()
    stores.append(copy)
    cosine = inner / jnp.sqrt((proj_sq + 1e-06) * (target_sq + 1e-06))
    cos_out[...] = jnp.broadcast_to(cosine, (rows, rows)).T[0:1, :]
    for copy in stores:
        copy.wait()


def fused_device(
    query_rows,
    key_rows,
    value_rows,
    residual,
    out_weight,
    proj_first,
    proj_second,
    dino_feats,
    slot_frame,
    patch_taps,
):
    seq_count = lax.axis_size("seq")
    rows, all_cols = query_rows.shape
    tokens, wide = residual.shape
    units = proj_first.shape[1]
    feats = proj_second.shape[1]
    width = CHUNK_HEADS * HD
    chunks = all_cols // 4 // width
    groups = ROW_GROUPS
    sub = rows // groups
    held, part_patches = dino_feats.shape[:2]
    bf16 = jnp.bfloat16
    f32 = jnp.float32
    dma = pltpu.SemaphoreType.DMA
    any_spec = pl.BlockSpec(memory_space=pl.ANY)
    vmem_spec = pl.BlockSpec(memory_space=pltpu.VMEM)
    hidden, lifted, frames = pl.pallas_call(
        functools.partial(fused_kernel, seq_count),
        out_shape=(
            jax.ShapeDtypeStruct((4, groups, sub, wide), bf16),
            jax.ShapeDtypeStruct((rows, units), bf16),
            jax.ShapeDtypeStruct((4 * part_patches, feats), bf16),
        ),
        in_specs=[any_spec] * 7 + [pl.BlockSpec(memory_space=pltpu.SMEM)],
        out_specs=(any_spec, vmem_spec, vmem_spec),
        scratch_shapes=[
            pltpu.VMEM((chunks, groups, 4, sub, width), bf16),
            pltpu.VMEM((2, chunks, tokens, width), bf16),
            pltpu.VMEM((groups, 4 * sub, all_cols), bf16),
            pltpu.VMEM((4 * sub, wide), f32),
            pltpu.VMEM(out_weight.shape, bf16),
            pltpu.VMEM(proj_first.shape, bf16),
            pltpu.VMEM((groups, 4, sub, wide), bf16),
            pltpu.VMEM((groups, 4, sub, wide), bf16),
            pltpu.VMEM((groups, 4, sub, units), f32),
            pltpu.VMEM((groups, 2, sub, units), f32),
            pltpu.VMEM((groups, sub, units), bf16),
            pltpu.VMEM((groups, sub, units), bf16),
            pltpu.VMEM((seq_count, held, part_patches, feats), bf16),
            pltpu.VMEM((held, part_patches, feats), bf16),
            pltpu.VMEM((4, part_patches, feats), bf16),
            dma((3,)),
            dma((groups,)),
            dma((3, chunks)),
            dma((3, 3, chunks)),
            dma((3, 3, chunks)),
            dma((groups, 2)),
            dma((groups, 2)),
            dma((groups, 2)),
            dma((groups, 2)),
            dma((groups,)),
            dma((groups,)),
            dma((groups, 2)),
            dma((groups, 2)),
            dma((groups,)),
            dma((groups,)),
            dma((seq_count - 1,)),
            dma((seq_count - 1,)),
            dma((3,)),
            dma((3,)),
            dma((groups,)),
        ],
        compiler_params=pltpu.CompilerParams(
            collective_id=0, has_side_effects=True, vmem_limit_bytes=56 * 1024 * 1024
        ),
        cost_estimate=pl.CostEstimate(
            flops=2 * tokens * (all_cols * wide + wide * units),
            bytes_accessed=24 * 1024 * 1024,
            transcendentals=0,
        ),
        name="sublayer",
    )(
        query_rows.reshape(groups, sub, all_cols),
        key_rows,
        value_rows,
        residual.reshape(4, groups, sub, wide),
        out_weight,
        proj_first,
        dino_feats,
        slot_frame,
    )
    hidden, projected, target, cosine = pl.pallas_call(
        project_kernel,
        out_shape=(
            jax.ShapeDtypeStruct(hidden.shape, bf16),
            jax.ShapeDtypeStruct((rows, feats), bf16),
            jax.ShapeDtypeStruct((rows, feats), f32),
            jax.ShapeDtypeStruct((1, rows), f32),
        ),
        in_specs=[any_spec, vmem_spec, vmem_spec, vmem_spec, any_spec],
        out_specs=(any_spec, any_spec, any_spec, vmem_spec),
        scratch_shapes=[
            pltpu.VMEM(hidden.shape, bf16),
            pltpu.VMEM(proj_second.shape, bf16),
            pltpu.VMEM((rows, feats), bf16),
            pltpu.VMEM((rows, feats), f32),
            dma((4,)),
            dma((4,)),
            dma((feats // 256,)),
            dma((2,)),
        ],
        compiler_params=pltpu.CompilerParams(vmem_limit_bytes=56 * 1024 * 1024),
        cost_estimate=pl.CostEstimate(
            flops=2 * rows * units * feats, bytes_accessed=8 * 1024 * 1024, transcendentals=0
        ),
        name="project",
    )(hidden, lifted, frames, patch_taps.T, proj_second)
    return (hidden.reshape(tokens, wide), projected, target, cosine.reshape(rows))


def solution(mesh):
    body = fused_device if mesh.shape["head"] == 4 else per_device
    return jax.shard_map(
        body,
        mesh=mesh,
        in_specs=(
            P(("seq", "head"), None),
            P(("seq", "head"), None),
            P(("seq", "head"), None),
            P("seq", "head"),
            P(None, "head"),
            P("head", None),
            P(),
            P("seq", "head", None),
            P(),
            P(("seq", "head"), None),
        ),
        out_specs=(
            P("seq", "head"),
            P(("seq", "head"), None),
            P(("seq", "head"), None),
            P(("seq", "head")),
        ),
        check_vma=False,
    )
```

```python
import functools

import jax
import jax.numpy as jnp
from jax import lax
from jax.experimental import pallas as pl
from jax.experimental.pallas import tpu as pltpu
from jax.sharding import PartitionSpec as P

HD = 128
PPF = 64
TAPS = 4
BLOCK = 512


def attend(operands):
    query_part, key_part, value_part = operands
    length = query_part.shape[0]
    item_count = query_part.shape[2]
    window_count = length // BLOCK
    score_scale = HD ** (-0.5)
    shaped = (
        query_part[:, 0].reshape(window_count, BLOCK, item_count, HD),
        key_part[:, 0].reshape(window_count, BLOCK, item_count, HD),
        value_part[:, 0].reshape(window_count, BLOCK, item_count, HD),
    )

    def one_window(parts):
        query_block, key_block, value_block = parts
        scores = (
            jnp.einsum("qhd,khd->hqk", query_block, key_block, preferred_element_type=jnp.float32)
            * score_scale
        )
        row_max = jnp.max(scores, axis=-1, keepdims=True)
        exponents = jnp.exp(scores - row_max)
        weights = (exponents / jnp.sum(exponents, axis=-1, keepdims=True)).astype(jnp.bfloat16)
        return jnp.einsum(
            "hqk,khd->qhd", weights, value_block, preferred_element_type=jnp.float32
        ).astype(jnp.bfloat16)

    return lax.map(one_window, shaped).reshape(length, 1, item_count, HD)


def per_device(
    query_rows,
    key_rows,
    value_rows,
    residual,
    out_weight,
    proj_first,
    proj_second,
    dino_feats,
    slot_frame,
    patch_taps,
):
    own_rows = query_rows.shape[0]
    group_count = lax.axis_size("head")
    per_group = query_rows.shape[1] // (HD * group_count)
    query_heads = query_rows.reshape(own_rows, group_count, per_group, HD)
    key_heads = key_rows.reshape(own_rows, group_count, per_group, HD)
    value_heads = value_rows.reshape(own_rows, group_count, per_group, HD)
    attended = attend(
        (
            lax.all_to_all(query_heads, "head", split_axis=1, concat_axis=0, tiled=True),
            lax.all_to_all(key_heads, "head", split_axis=1, concat_axis=0, tiled=True),
            lax.all_to_all(value_heads, "head", split_axis=1, concat_axis=0, tiled=True),
        )
    )
    seq_len = attended.shape[0]
    attended = attended.reshape(seq_len, per_group * HD)
    mixed_sum = jnp.dot(
        lax.all_gather(attended, "head", axis=1, tiled=True),
        out_weight,
        preferred_element_type=jnp.float32,
    )
    hidden = (residual.astype(jnp.float32) + mixed_sum).astype(jnp.bfloat16)
    pre_act = lax.psum_scatter(
        jnp.dot(hidden, proj_first, preferred_element_type=jnp.float32),
        "head",
        scatter_dimension=0,
        tiled=True,
    )
    lifted = jax.nn.silu(pre_act).astype(jnp.bfloat16)
    projected = jnp.dot(lifted, proj_second, preferred_element_type=jnp.float32).astype(
        jnp.bfloat16
    )
    seq_index = lax.axis_index("seq")
    head_index = lax.axis_index("head")
    frames_here = dino_feats.shape[0]
    wanted = seq_index * frames_here + jnp.arange(frames_here, dtype=jnp.int32)
    everything = lax.all_gather(dino_feats, "seq", axis=0, tiled=True)
    picker = (slot_frame[None, :] == wanted[:, None]).astype(jnp.bfloat16)
    frame_part = jnp.einsum(
        "ir,rpz->ipz", picker, everything, preferred_element_type=jnp.float32
    ).astype(jnp.bfloat16)
    whole_frames = lax.all_gather(frame_part, "head", axis=1, tiled=True)
    frame_feat = lax.dynamic_index_in_dim(whole_frames, head_index // 2, 0, keepdims=False)
    patch_ids = jnp.arange(PPF, dtype=jnp.int32)
    tap_counts = jnp.sum(
        (patch_taps[:, :, None] == patch_ids[None, None, :]).astype(jnp.float32), axis=1
    )
    target = jnp.dot(
        tap_counts.astype(jnp.bfloat16), frame_feat, preferred_element_type=jnp.float32
    ) * (1.0 / TAPS)
    proj_float = projected.astype(jnp.float32)
    inner = jnp.sum(proj_float * target, axis=-1)
    proj_sq = jnp.sum(proj_float * proj_float, axis=-1) + 1e-06
    target_sq = jnp.sum(target * target, axis=-1) + 1e-06
    cosine = inner / jnp.sqrt(proj_sq * target_sq)
    return (hidden, projected, target, cosine)


CHUNK_HEADS = 2
ROW_GROUPS = 4
MESH = pl.DeviceIdType.MESH


def fused_kernel(
    seq_count,
    q_ref,
    k_ref,
    v_ref,
    res_ref,
    w_ref,
    p1_ref,
    p2_ref,
    dino_ref,
    slot_ref,
    taps_ref,
    hid_out,
    proj_out,
    targ_out,
    cos_out,
    q_buf,
    kv_buf,
    att,
    acc,
    w_v,
    p1_v,
    p2_v,
    res_v,
    hid_v,
    pre_v,
    lift_v,
    sib_part,
    cross_send,
    cross_part,
    dino_all,
    frame_sel,
    frame_buf,
    load_sem,
    res_sem,
    own_sem,
    qkv_send,
    qkv_recv,
    sib_send,
    sib_recv,
    cross_ssem,
    cross_rsem,
    fwd_send,
    fwd_recv,
    part_send,
    part_recv,
    hop_send,
    hop_recv,
    dino_send,
    dino_recv,
    frame_send,
    frame_recv,
    hid_sem,
):
    seq = lax.axis_index("seq")
    me = lax.axis_index("head")
    chip = lax.div(me, 2)
    core = lax.rem(me, 2)
    sib = 2 * chip + (1 - core)
    cross = 2 * (1 - chip) + core
    diag = 2 * (1 - chip) + (1 - core)
    peers = (sib, cross, diag)
    groups, sub, all_cols = q_ref.shape
    rows = groups * sub
    tokens = 4 * rows
    group_rows = 4 * sub
    head_cols = all_cols // 4
    chunks = q_buf.shape[0]
    width = q_buf.shape[4]
    heads = width // HD
    wide = w_v.shape[1]
    units = p1_v.shape[1]
    tile = 256

    barrier = pltpu.get_barrier_semaphore()
    for peer in peers:
        pl.semaphore_signal(barrier, inc=1, device_id={"head": peer}, device_id_type=MESH)
    for step in range(1, seq_count):
        other = lax.rem(seq + step, seq_count)
        pl.semaphore_signal(barrier, inc=1, device_id={"seq": other}, device_id_type=MESH)
    pl.semaphore_wait(barrier, 3 + seq_count - 1)

    def send(src, dst, ssem, rsem, peer):
        copy = pltpu.make_async_remote_copy(
            src_ref=src,
            dst_ref=dst,
            send_sem=ssem,
            recv_sem=rsem,
            device_id={"head": peer},
            device_id_type=MESH,
        )
        copy.start()
        return copy

    my_rows = pl.ds(pl.multiple_of(me * rows, rows), rows)

    def columns(owner, i):
        return pl.ds(pl.multiple_of(owner * head_cols + i * width, width), width)

    def source(t, owner, i):
        if t == 0:
            return q_ref.at[:, :, columns(owner, i)]
        return (k_ref, v_ref)[t - 1].at[:, columns(owner, i)]

    def landing(t, i):
        if t == 0:
            return q_buf.at[i, :, me]
        return kv_buf.at[t - 1, i, my_rows, :]

    qkv_copies = {}
    own_copies = {}

    def send_chunk(i):
        for t in range(3):
            for m in (2, 1, 0):
                qkv_copies[t, m, i] = send(
                    source(t, peers[m], i),
                    landing(t, i),
                    qkv_send.at[t, m, i],
                    qkv_recv.at[t, m, i],
                    peers[m],
                )
            copy = pltpu.make_async_copy(source(t, me, i), landing(t, i), own_sem.at[t, i])
            copy.start()
            own_copies[t, i] = copy

    ahead = min(2, chunks)
    for i in range(ahead):
        send_chunk(i)

    dino_copies = []
    for step in range(1, seq_count):
        copy = pltpu.make_async_remote_copy(
            src_ref=dino_ref,
            dst_ref=dino_all.at[seq],
            send_sem=dino_send.at[step - 1],
            recv_sem=dino_recv.at[step - 1],
            device_id={"seq": lax.rem(seq + step, seq_count)},
            device_id_type=MESH,
        )
        copy.start()
        dino_copies.append(copy)
    loads = []
    for n, (src, dst) in enumerate(
        ((dino_ref, dino_all.at[seq]), (w_ref, w_v), (p1_ref, p1_v), (p2_ref, p2_v))
    ):
        copy = pltpu.make_async_copy(src, dst, load_sem.at[n])
        copy.start()
        loads.append(copy)
    res_loads = []
    for g in range(groups):
        copy = pltpu.make_async_copy(res_ref.at[:, g], res_v.at[g], res_sem.at[g])
        copy.start()
        res_loads.append(copy)

    score_scale = HD ** (-0.5)

    def attend(i, n, first, count):
        lanes = pl.ds(pl.multiple_of(n * HD, HD), HD)
        query = q_buf[i, pl.ds(first, count), :, :, lanes].reshape(count * group_rows, HD)
        scores = lax.dot_general(
            query,
            kv_buf[0, i, :, lanes],
            (((1,), (1,)), ((), ())),
            preferred_element_type=jnp.float32,
        )
        scores = scores * score_scale
        top = jnp.max(scores, axis=-1, keepdims=True)
        exponents = jnp.exp(scores - top)
        total = jnp.sum(exponents, axis=-1, keepdims=True)
        mixed = jnp.dot(
            exponents.astype(jnp.bfloat16),
            kv_buf[1, i, :, lanes],
            preferred_element_type=jnp.float32,
        )
        mixed = (mixed / total).astype(jnp.bfloat16)
        place = pl.ds(pl.multiple_of(me * head_cols + i * width + n * HD, HD), HD)
        att[pl.ds(first, count), :, place] = mixed.reshape(count, group_rows, HD)

    both = min(2, groups)

    def attend_chunk(i):
        def body(n, carry):
            attend(i, lax.div(n, groups // both), lax.rem(n, groups // both) * both, both)
            return carry

        lax.fori_loop(0, heads * (groups // both), body, 0)

    last = chunks - 1
    early = last * width

    def owned(g, owner, start, size):
        return att.at[g, :, pl.ds(pl.multiple_of(owner * head_cols + start, width), size)]

    att_copies = {}

    def send_att(g, part):
        if part == 0:
            mine = owned(g, me, 0, early)
        elif g == 0:
            mine = owned(g, me, early, width)
        else:
            mine = owned(g, me, 0, head_cols)
        att_copies[1, g, part] = send(
            mine, mine, cross_ssem.at[g, part], cross_rsem.at[g, part], cross
        )
        att_copies[0, g, part] = send(mine, mine, sib_send.at[g, part], sib_recv.at[g, part], sib)

    frame_copies = []

    def pick_frames():
        for copy in dino_copies:
            copy.wait_recv()
        loads[0].wait()
        held = dino_ref.shape[0]
        for f in range(frame_sel.shape[0]):
            total = jnp.zeros(frame_sel.shape[1:], jnp.float32)
            for r in range(seq_count * held):
                hit = (slot_ref[r] == seq * held + f).astype(jnp.float32)
                total = total + hit * dino_all[r // held, r % held].astype(jnp.float32)
            frame_sel[f] = total.astype(jnp.bfloat16)
        for m, (peer, which) in enumerate(((sib, chip), (cross, 1 - chip))):
            frame_copies.append(
                send(
                    frame_sel.at[which],
                    frame_buf.at[me],
                    frame_send.at[m],
                    frame_recv.at[m],
                    peer,
                )
            )
        frame_buf[me] = frame_sel[chip]

    def forward_frames():
        frame_copies[1].wait_recv()
        frame_copies.append(
            send(
                frame_buf.at[cross], frame_buf.at[cross], frame_send.at[2], frame_recv.at[2], sib
            )
        )

    def make_target():
        frame_copies[0].wait_recv()
        frame_copies[2].wait_recv()
        patches = lax.broadcasted_iota(jnp.int32, (PPF, rows), 0)
        counts = jnp.zeros((PPF, rows), jnp.float32)
        for t in range(TAPS):
            counts = counts + (taps_ref[t : t + 1, :] == patches).astype(jnp.float32)
        counts = counts.T.astype(jnp.bfloat16)
        frame = frame_buf[...].reshape(PPF, frame_buf.shape[2])
        targ_out[...] = jnp.dot(counts, frame, preferred_element_type=jnp.float32) * (1.0 / TAPS)

    for i in range(last):
        for t in range(3):
            for m in range(3):
                qkv_copies[t, m, i].wait_recv()
            own_copies[t, i].wait()
        if i + ahead < chunks:
            send_chunk(i + ahead)
        attend_chunk(i)
    send_att(0, 0)
    for t in range(3):
        for m in range(3):
            qkv_copies[t, m, last].wait_recv()
        own_copies[t, last].wait()
    for g in range(groups):

        def last_heads(n, carry, g=g):
            attend(last, n, g, 1)
            return carry

        lax.fori_loop(0, heads, last_heads, 0)
        send_att(g, 1)
    pick_frames()
    loads[1].wait()

    def products(g, owners, cols):
        total = None
        for owner in owners:
            part = pl.ds(pl.multiple_of(owner * head_cols, head_cols), head_cols)
            term = jnp.dot(
                att[g, :, part], w_v[part, cols], preferred_element_type=jnp.float32
            )
            total = term if total is None else total + term
        return total

    def over_tiles(count, step):
        def body(n, carry):
            step(pl.ds(pl.multiple_of(n * tile, tile), tile))
            return carry

        lax.fori_loop(0, count // tile, body, 0)

    hid_copies = []
    part_copies = {}
    hop_copies = {}
    fwd_copies = {}

    def reduce_hop(g):
        part_copies[g, 0].wait_recv()
        cross_send[g] = (pre_v[g, cross] + sib_part[g, 0]).astype(jnp.bfloat16)
        hop_copies[g] = send(
            cross_send.at[g], cross_part.at[g], hop_send.at[g], hop_recv.at[g], cross
        )

    for g in range(groups):
        for part in (0, 1) if g == 0 else (1,):
            att_copies[0, g, part].wait_recv()

        def near(cols, g=g):
            acc[:, cols] = products(g, (me, sib), cols)

        over_tiles(wide, near)
        if g >= 1:
            reduce_hop(g - 1)
        for part in (0, 1) if g == 0 else (1,):
            att_copies[1, g, part].wait_recv()
        theirs = owned(g, cross, 0, head_cols)
        fwd_copies[g] = send(theirs, theirs, fwd_send.at[g], fwd_recv.at[g], sib)

        def far(cols, g=g):
            acc[:, cols] = acc[:, cols] + products(g, (cross,), cols)

        over_tiles(wide, far)
        fwd_copies[g].wait_recv()
        res_loads[g].wait()

        def close(cols, g=g):
            total = acc[:, cols] + products(g, (diag,), cols)
            total = total.reshape(4, sub, tile) + res_v[g, :, :, cols].astype(jnp.float32)
            hid_v[g, :, :, cols] = total.astype(jnp.bfloat16)

        over_tiles(wide, close)
        copy = pltpu.make_async_copy(hid_v.at[g], hid_out.at[:, g], hid_sem.at[g])
        copy.start()
        hid_copies.append(copy)
        if g == 0:
            loads[2].wait()

        def first_layer(cols, g=g):
            value = jnp.dot(
                hid_v[g].reshape(group_rows, wide), p1_v[:, cols],
                preferred_element_type=jnp.float32,
            )
            pre_v[g, :, :, cols] = value.reshape(4, sub, tile)

        over_tiles(units, first_layer)
        for n, owner in enumerate((diag, sib)):
            part_copies[g, n] = send(
                pre_v.at[g, owner],
                sib_part.at[g, n],
                part_send.at[g, n],
                part_recv.at[g, n],
                sib,
            )
    forward_frames()
    reduce_hop(groups - 1)
    loads[3].wait()
    make_target()
    for g in range(groups):
        part_copies[g, 1].wait_recv()
        hop_copies[g].wait_recv()
        pre_act = pre_v[g, me] + sib_part[g, 1] + cross_part[g].astype(jnp.float32)
        lift_v[pl.ds(g * sub, sub), :] = (pre_act / (1.0 + jnp.exp(-pre_act))).astype(
            jnp.bfloat16
        )

    def project(n, sums):
        cols = pl.ds(pl.multiple_of(n * tile, tile), tile)
        value = jnp.dot(lift_v[...], p2_v[:, cols], preferred_element_type=jnp.float32).astype(
            jnp.bfloat16
        )
        proj_out[:, cols] = value
        value = value.astype(jnp.float32)
        target = targ_out[:, cols]
        inner, proj_sq, target_sq = sums
        return (
            inner + jnp.sum(value * target, axis=-1, keepdims=True),
            proj_sq + jnp.sum(value * value, axis=-1, keepdims=True),
            target_sq + jnp.sum(target * target, axis=-1, keepdims=True),
        )

    zero = jnp.zeros((rows, 1), jnp.float32)
    inner, proj_sq, target_sq = lax.fori_loop(
        0, p2_v.shape[1] // tile, project, (zero, zero, zero)
    )
    cosine = inner / jnp.sqrt((proj_sq + 1e-06) * (target_sq + 1e-06))
    cos_out[...] = jnp.broadcast_to(cosine, (rows, rows)).T[0:1, :]

    for copy in hid_copies:
        copy.wait()
    for copies in (qkv_copies, att_copies, fwd_copies, part_copies, hop_copies):
        for copy in copies.values():
            copy.wait_send()
    for copy in dino_copies + frame_copies:
        copy.wait_send()


def place_kernel(hid, proj, targ, cos, hid_out, proj_out, targ_out, cos_out, hid_v, proj_v, targ_v, load_sem, store_sem):
    moves = [(hid.at[n], hid_v.at[n], hid_out.at[n]) for n in range(hid.shape[0])]
    moves += [(proj, proj_v, proj_out), (targ, targ_v, targ_out)]
    loads = [
        pltpu.make_async_copy(src, held, load_sem.at[n]) for n, (src, held, _) in enumerate(moves)
    ]
    stores = [
        pltpu.make_async_copy(held, dst, store_sem.at[n]) for n, (_, held, dst) in enumerate(moves)
    ]
    for load in loads:
        load.start()
    cos_out[...] = cos[...]
    for load, store in zip(loads, stores):
        load.wait()
        store.start()
    for store in stores:
        store.wait()


def fused_device(
    query_rows,
    key_rows,
    value_rows,
    residual,
    out_weight,
    proj_first,
    proj_second,
    dino_feats,
    slot_frame,
    patch_taps,
):
    seq_count = lax.axis_size("seq")
    rows, all_cols = query_rows.shape
    tokens, wide = residual.shape
    units = proj_first.shape[1]
    feats = proj_second.shape[1]
    width = CHUNK_HEADS * HD
    chunks = all_cols // 4 // width
    groups = ROW_GROUPS
    sub = rows // groups
    held, part_patches = dino_feats.shape[:2]
    bf16 = jnp.bfloat16
    f32 = jnp.float32
    dma = pltpu.SemaphoreType.DMA
    any_spec = pl.BlockSpec(memory_space=pl.ANY)
    vmem_spec = pl.BlockSpec(memory_space=pltpu.VMEM)
    hidden, projected, target, cosine = pl.pallas_call(
        functools.partial(fused_kernel, seq_count),
        out_shape=(
            jax.ShapeDtypeStruct((4, groups, sub, wide), bf16),
            jax.ShapeDtypeStruct((rows, feats), bf16),
            jax.ShapeDtypeStruct((rows, feats), f32),
            jax.ShapeDtypeStruct((1, rows), f32),
        ),
        in_specs=[any_spec] * 8 + [pl.BlockSpec(memory_space=pltpu.SMEM), vmem_spec],
        out_specs=(any_spec, vmem_spec, vmem_spec, vmem_spec),
        scratch_shapes=[
            pltpu.VMEM((chunks, groups, 4, sub, width), bf16),
            pltpu.VMEM((2, chunks, tokens, width), bf16),
            pltpu.VMEM((groups, 4 * sub, all_cols), bf16),
            pltpu.VMEM((4 * sub, wide), f32),
            pltpu.VMEM(out_weight.shape, bf16),
            pltpu.VMEM(proj_first.shape, bf16),
            pltpu.VMEM(proj_second.shape, bf16),
            pltpu.VMEM((groups, 4, sub, wide), bf16),
            pltpu.VMEM((groups, 4, sub, wide), bf16),
            pltpu.VMEM((groups, 4, sub, units), f32),
            pltpu.VMEM((rows, units), bf16),
            pltpu.VMEM((groups, 2, sub, units), f32),
            pltpu.VMEM((groups, sub, units), bf16),
            pltpu.VMEM((groups, sub, units), bf16),
            pltpu.VMEM((seq_count, held, part_patches, feats), bf16),
            pltpu.VMEM((held, part_patches, feats), bf16),
            pltpu.VMEM((4, part_patches, feats), bf16),
            dma((4,)),
            dma((groups,)),
            dma((3, chunks)),
            dma((3, 3, chunks)),
            dma((3, 3, chunks)),
            dma((groups, 2)),
            dma((groups, 2)),
            dma((groups, 2)),
            dma((groups, 2)),
            dma((groups,)),
            dma((groups,)),
            dma((groups, 2)),
            dma((groups, 2)),
            dma((groups,)),
            dma((groups,)),
            dma((seq_count - 1,)),
            dma((seq_count - 1,)),
            dma((3,)),
            dma((3,)),
            dma((groups,)),
        ],
        compiler_params=pltpu.CompilerParams(
            collective_id=0, has_side_effects=True, vmem_limit_bytes=56 * 1024 * 1024
        ),
        cost_estimate=pl.CostEstimate(
            flops=2 * tokens * (all_cols * wide + wide * units),
            bytes_accessed=24 * 1024 * 1024,
            transcendentals=0,
        ),
        name="sublayer",
    )(
        query_rows.reshape(groups, sub, all_cols),
        key_rows,
        value_rows,
        residual.reshape(4, groups, sub, wide),
        out_weight,
        proj_first,
        proj_second,
        dino_feats,
        slot_frame,
        patch_taps.T,
    )
    parts = (hidden, projected, target, cosine)
    hidden, projected, target, cosine = pl.pallas_call(
        place_kernel,
        out_shape=tuple(jax.ShapeDtypeStruct(part.shape, part.dtype) for part in parts),
        in_specs=[any_spec] * 3 + [vmem_spec],
        out_specs=(any_spec,) * 3 + (vmem_spec,),
        scratch_shapes=[
            pltpu.VMEM(hidden.shape, bf16),
            pltpu.VMEM((rows, feats), bf16),
            pltpu.VMEM((rows, feats), f32),
            dma((6,)),
            dma((6,)),
        ],
        compiler_params=pltpu.CompilerParams(vmem_limit_bytes=56 * 1024 * 1024),
        name="place",
    )(*parts)
    return (hidden.reshape(tokens, wide), projected, target, cosine.reshape(rows))


def solution(mesh):
    body = fused_device if mesh.shape["head"] == 4 else per_device
    return jax.shard_map(
        body,
        mesh=mesh,
        in_specs=(
            P(("seq", "head"), None),
            P(("seq", "head"), None),
            P(("seq", "head"), None),
            P("seq", "head"),
            P(None, "head"),
            P("head", None),
            P(),
            P("seq", "head", None),
            P(),
            P(("seq", "head"), None),
        ),
        out_specs=(
            P("seq", "head"),
            P(("seq", "head"), None),
            P(("seq", "head"), None),
            P(("seq", "head")),
        ),
        check_vma=False,
    )
```

```python
import functools

import jax
import jax.numpy as jnp
from jax import lax
from jax.experimental import pallas as pl
from jax.experimental.pallas import tpu as pltpu
from jax.sharding import PartitionSpec as P

HD = 128
PPF = 64
TAPS = 4
BLOCK = 512


def attend(operands):
    query_part, key_part, value_part = operands
    length = query_part.shape[0]
    item_count = query_part.shape[2]
    window_count = length // BLOCK
    score_scale = HD ** (-0.5)
    shaped = (
        query_part[:, 0].reshape(window_count, BLOCK, item_count, HD),
        key_part[:, 0].reshape(window_count, BLOCK, item_count, HD),
        value_part[:, 0].reshape(window_count, BLOCK, item_count, HD),
    )

    def one_window(parts):
        query_block, key_block, value_block = parts
        scores = (
            jnp.einsum("qhd,khd->hqk", query_block, key_block, preferred_element_type=jnp.float32)
            * score_scale
        )
        row_max = jnp.max(scores, axis=-1, keepdims=True)
        exponents = jnp.exp(scores - row_max)
        weights = (exponents / jnp.sum(exponents, axis=-1, keepdims=True)).astype(jnp.bfloat16)
        return jnp.einsum(
            "hqk,khd->qhd", weights, value_block, preferred_element_type=jnp.float32
        ).astype(jnp.bfloat16)

    return lax.map(one_window, shaped).reshape(length, 1, item_count, HD)


def per_device(
    query_rows,
    key_rows,
    value_rows,
    residual,
    out_weight,
    proj_first,
    proj_second,
    dino_feats,
    slot_frame,
    patch_taps,
):
    own_rows = query_rows.shape[0]
    group_count = lax.axis_size("head")
    per_group = query_rows.shape[1] // (HD * group_count)
    query_heads = query_rows.reshape(own_rows, group_count, per_group, HD)
    key_heads = key_rows.reshape(own_rows, group_count, per_group, HD)
    value_heads = value_rows.reshape(own_rows, group_count, per_group, HD)
    attended = attend(
        (
            lax.all_to_all(query_heads, "head", split_axis=1, concat_axis=0, tiled=True),
            lax.all_to_all(key_heads, "head", split_axis=1, concat_axis=0, tiled=True),
            lax.all_to_all(value_heads, "head", split_axis=1, concat_axis=0, tiled=True),
        )
    )
    seq_len = attended.shape[0]
    attended = attended.reshape(seq_len, per_group * HD)
    mixed_sum = jnp.dot(
        lax.all_gather(attended, "head", axis=1, tiled=True),
        out_weight,
        preferred_element_type=jnp.float32,
    )
    hidden = (residual.astype(jnp.float32) + mixed_sum).astype(jnp.bfloat16)
    pre_act = lax.psum_scatter(
        jnp.dot(hidden, proj_first, preferred_element_type=jnp.float32),
        "head",
        scatter_dimension=0,
        tiled=True,
    )
    lifted = jax.nn.silu(pre_act).astype(jnp.bfloat16)
    projected = jnp.dot(lifted, proj_second, preferred_element_type=jnp.float32).astype(
        jnp.bfloat16
    )
    seq_index = lax.axis_index("seq")
    head_index = lax.axis_index("head")
    frames_here = dino_feats.shape[0]
    wanted = seq_index * frames_here + jnp.arange(frames_here, dtype=jnp.int32)
    everything = lax.all_gather(dino_feats, "seq", axis=0, tiled=True)
    picker = (slot_frame[None, :] == wanted[:, None]).astype(jnp.bfloat16)
    frame_part = jnp.einsum(
        "ir,rpz->ipz", picker, everything, preferred_element_type=jnp.float32
    ).astype(jnp.bfloat16)
    whole_frames = lax.all_gather(frame_part, "head", axis=1, tiled=True)
    frame_feat = lax.dynamic_index_in_dim(whole_frames, head_index // 2, 0, keepdims=False)
    patch_ids = jnp.arange(PPF, dtype=jnp.int32)
    tap_counts = jnp.sum(
        (patch_taps[:, :, None] == patch_ids[None, None, :]).astype(jnp.float32), axis=1
    )
    target = jnp.dot(
        tap_counts.astype(jnp.bfloat16), frame_feat, preferred_element_type=jnp.float32
    ) * (1.0 / TAPS)
    proj_float = projected.astype(jnp.float32)
    inner = jnp.sum(proj_float * target, axis=-1)
    proj_sq = jnp.sum(proj_float * proj_float, axis=-1) + 1e-06
    target_sq = jnp.sum(target * target, axis=-1) + 1e-06
    cosine = inner / jnp.sqrt(proj_sq * target_sq)
    return (hidden, projected, target, cosine)


CHUNK_HEADS = 2
ROW_GROUPS = 4
MESH = pl.DeviceIdType.MESH


def fused_kernel(
    seq_count,
    q_ref,
    k_ref,
    v_ref,
    res_ref,
    w_ref,
    p1_ref,
    p2_ref,
    dino_ref,
    slot_ref,
    taps_ref,
    hid_out,
    proj_out,
    targ_out,
    cos_out,
    q_buf,
    kv_buf,
    att,
    acc,
    w_v,
    p1_v,
    p2_v,
    res_v,
    hid_v,
    pre_v,
    lift_v,
    sib_part,
    cross_send,
    cross_part,
    dino_all,
    frame_sel,
    frame_buf,
    load_sem,
    res_sem,
    own_sem,
    qkv_send,
    qkv_recv,
    sib_send,
    sib_recv,
    cross_ssem,
    cross_rsem,
    fwd_send,
    fwd_recv,
    part_send,
    part_recv,
    hop_send,
    hop_recv,
    dino_send,
    dino_recv,
    frame_send,
    frame_recv,
    hid_sem,
):
    seq = lax.axis_index("seq")
    me = lax.axis_index("head")
    chip = lax.div(me, 2)
    core = lax.rem(me, 2)
    sib = 2 * chip + (1 - core)
    cross = 2 * (1 - chip) + core
    diag = 2 * (1 - chip) + (1 - core)
    peers = (sib, cross, diag)
    groups, sub, all_cols = q_ref.shape
    rows = groups * sub
    tokens = 4 * rows
    group_rows = 4 * sub
    head_cols = all_cols // 4
    chunks = q_buf.shape[0]
    width = q_buf.shape[4]
    heads = width // HD
    wide = w_v.shape[1]
    units = p1_v.shape[1]
    tile = 256

    barrier = pltpu.get_barrier_semaphore()
    for peer in peers:
        pl.semaphore_signal(barrier, inc=1, device_id={"head": peer}, device_id_type=MESH)
    for step in range(1, seq_count):
        other = lax.rem(seq + step, seq_count)
        pl.semaphore_signal(barrier, inc=1, device_id={"seq": other}, device_id_type=MESH)
    pl.semaphore_wait(barrier, 3 + seq_count - 1)

    def send(src, dst, ssem, rsem, peer):
        copy = pltpu.make_async_remote_copy(
            src_ref=src,
            dst_ref=dst,
            send_sem=ssem,
            recv_sem=rsem,
            device_id={"head": peer},
            device_id_type=MESH,
        )
        copy.start()
        return copy

    my_rows = pl.ds(pl.multiple_of(me * rows, rows), rows)

    def columns(owner, i):
        return pl.ds(pl.multiple_of(owner * head_cols + i * width, width), width)

    def source(t, owner, i):
        if t == 0:
            return q_ref.at[:, :, columns(owner, i)]
        return (k_ref, v_ref)[t - 1].at[:, columns(owner, i)]

    def landing(t, i):
        if t == 0:
            return q_buf.at[i, :, me]
        return kv_buf.at[t - 1, i, my_rows, :]

    qkv_copies = {}
    own_copies = {}

    def send_chunk(i):
        for t in range(3):
            for m in (2, 1, 0):
                qkv_copies[t, m, i] = send(
                    source(t, peers[m], i),
                    landing(t, i),
                    qkv_send.at[t, m, i],
                    qkv_recv.at[t, m, i],
                    peers[m],
                )
            copy = pltpu.make_async_copy(source(t, me, i), landing(t, i), own_sem.at[t, i])
            copy.start()
            own_copies[t, i] = copy

    ahead = min(2, chunks)
    for i in range(ahead):
        send_chunk(i)

    dino_copies = []
    for step in range(1, seq_count):
        copy = pltpu.make_async_remote_copy(
            src_ref=dino_ref,
            dst_ref=dino_all.at[seq],
            send_sem=dino_send.at[step - 1],
            recv_sem=dino_recv.at[step - 1],
            device_id={"seq": lax.rem(seq + step, seq_count)},
            device_id_type=MESH,
        )
        copy.start()
        dino_copies.append(copy)
    loads = []
    for n, (src, dst) in enumerate(
        ((dino_ref, dino_all.at[seq]), (w_ref, w_v), (p1_ref, p1_v), (p2_ref, p2_v))
    ):
        copy = pltpu.make_async_copy(src, dst, load_sem.at[n])
        copy.start()
        loads.append(copy)
    res_loads = []
    for g in range(groups):
        copy = pltpu.make_async_copy(res_ref.at[:, g], res_v.at[g], res_sem.at[g])
        copy.start()
        res_loads.append(copy)

    score_scale = HD ** (-0.5)

    def attend(i, n, first, count):
        lanes = pl.ds(pl.multiple_of(n * HD, HD), HD)
        query = q_buf[i, pl.ds(first, count), :, :, lanes].reshape(count * group_rows, HD)
        scores = lax.dot_general(
            query,
            kv_buf[0, i, :, lanes],
            (((1,), (1,)), ((), ())),
            preferred_element_type=jnp.float32,
        )
        scores = scores * score_scale
        top = jnp.max(scores, axis=-1, keepdims=True)
        exponents = jnp.exp(scores - top)
        total = jnp.sum(exponents, axis=-1, keepdims=True)
        mixed = jnp.dot(
            exponents.astype(jnp.bfloat16),
            kv_buf[1, i, :, lanes],
            preferred_element_type=jnp.float32,
        )
        mixed = (mixed / total).astype(jnp.bfloat16)
        place = pl.ds(pl.multiple_of(me * head_cols + i * width + n * HD, HD), HD)
        att[pl.ds(first, count), :, place] = mixed.reshape(count, group_rows, HD)

    both = min(2, groups)

    def attend_chunk(i):
        def body(n, carry):
            attend(i, lax.div(n, groups // both), lax.rem(n, groups // both) * both, both)
            return carry

        lax.fori_loop(0, heads * (groups // both), body, 0)

    last = chunks - 1
    early = last * width

    def owned(g, owner, start, size):
        return att.at[g, :, pl.ds(pl.multiple_of(owner * head_cols + start, width), size)]

    att_copies = {}

    def send_att(g, part):
        if part == 0:
            mine = owned(g, me, 0, early)
        elif g == 0:
            mine = owned(g, me, early, width)
        else:
            mine = owned(g, me, 0, head_cols)
        att_copies[1, g, part] = send(
            mine, mine, cross_ssem.at[g, part], cross_rsem.at[g, part], cross
        )
        att_copies[0, g, part] = send(mine, mine, sib_send.at[g, part], sib_recv.at[g, part], sib)

    frame_copies = []

    def pick_frames():
        for copy in dino_copies:
            copy.wait_recv()
        loads[0].wait()
        held = dino_ref.shape[0]
        for f in range(frame_sel.shape[0]):
            total = jnp.zeros(frame_sel.shape[1:], jnp.float32)
            for r in range(seq_count * held):
                hit = (slot_ref[r] == seq * held + f).astype(jnp.float32)
                total = total + hit * dino_all[r // held, r % held].astype(jnp.float32)
            frame_sel[f] = total.astype(jnp.bfloat16)
        for m, (peer, which) in enumerate(((sib, chip), (cross, 1 - chip))):
            frame_copies.append(
                send(
                    frame_sel.at[which],
                    frame_buf.at[me],
                    frame_send.at[m],
                    frame_recv.at[m],
                    peer,
                )
            )
        frame_buf[me] = frame_sel[chip]

    def forward_frames():
        frame_copies[1].wait_recv()
        frame_copies.append(
            send(
                frame_buf.at[cross], frame_buf.at[cross], frame_send.at[2], frame_recv.at[2], sib
            )
        )

    def make_target():
        frame_copies[0].wait_recv()
        frame_copies[2].wait_recv()
        patches = lax.broadcasted_iota(jnp.int32, (PPF, rows), 0)
        counts = jnp.zeros((PPF, rows), jnp.float32)
        for t in range(TAPS):
            counts = counts + (taps_ref[t : t + 1, :] == patches).astype(jnp.float32)
        counts = counts.T.astype(jnp.bfloat16)
        frame = frame_buf[...].reshape(PPF, frame_buf.shape[2])
        targ_out[...] = jnp.dot(counts, frame, preferred_element_type=jnp.float32) * (1.0 / TAPS)

    for i in range(last):
        for t in range(3):
            for m in range(3):
                qkv_copies[t, m, i].wait_recv()
            own_copies[t, i].wait()
        if i + ahead < chunks:
            send_chunk(i + ahead)
        attend_chunk(i)
    send_att(0, 0)
    for t in range(3):
        for m in range(3):
            qkv_copies[t, m, last].wait_recv()
        own_copies[t, last].wait()
    for g in range(groups):

        def last_heads(n, carry, g=g):
            attend(last, n, g, 1)
            return carry

        lax.fori_loop(0, heads, last_heads, 0)
        send_att(g, 1)
    pick_frames()
    loads[1].wait()

    def products(g, owners, cols):
        total = None
        for owner in owners:
            part = pl.ds(pl.multiple_of(owner * head_cols, head_cols), head_cols)
            term = jnp.dot(
                att[g, :, part], w_v[part, cols], preferred_element_type=jnp.float32
            )
            total = term if total is None else total + term
        return total

    def over_tiles(count, step):
        def body(n, carry):
            step(pl.ds(pl.multiple_of(n * tile, tile), tile))
            return carry

        lax.fori_loop(0, count // tile, body, 0)

    hid_copies = []
    part_copies = {}
    hop_copies = {}
    fwd_copies = {}

    def reduce_hop(g):
        part_copies[g, 0].wait_recv()
        cross_send[g] = (pre_v[g, cross] + sib_part[g, 0]).astype(jnp.bfloat16)
        hop_copies[g] = send(
            cross_send.at[g], cross_part.at[g], hop_send.at[g], hop_recv.at[g], cross
        )

    for g in range(groups):
        for part in (0, 1) if g == 0 else (1,):
            att_copies[0, g, part].wait_recv()

        def near(cols, g=g):
            acc[:, cols] = products(g, (me, sib), cols)

        over_tiles(wide, near)
        if g >= 1:
            reduce_hop(g - 1)
        for part in (0, 1) if g == 0 else (1,):
            att_copies[1, g, part].wait_recv()
        theirs = owned(g, cross, 0, head_cols)
        fwd_copies[g] = send(theirs, theirs, fwd_send.at[g], fwd_recv.at[g], sib)

        def far(cols, g=g):
            acc[:, cols] = acc[:, cols] + products(g, (cross,), cols)

        over_tiles(wide, far)
        fwd_copies[g].wait_recv()
        res_loads[g].wait()

        def close(cols, g=g):
            total = acc[:, cols] + products(g, (diag,), cols)
            total = total.reshape(4, sub, tile) + res_v[g, :, :, cols].astype(jnp.float32)
            hid_v[g, :, :, cols] = total.astype(jnp.bfloat16)

        over_tiles(wide, close)
        copy = pltpu.make_async_copy(hid_v.at[g], hid_out.at[:, g], hid_sem.at[g])
        copy.start()
        hid_copies.append(copy)
        if g == 0:
            loads[2].wait()

        def first_layer(cols, g=g):
            value = jnp.dot(
                hid_v[g].reshape(group_rows, wide), p1_v[:, cols],
                preferred_element_type=jnp.float32,
            )
            pre_v[g, :, :, cols] = value.reshape(4, sub, tile)

        over_tiles(units, first_layer)
        for n, owner in enumerate((diag, sib)):
            part_copies[g, n] = send(
                pre_v.at[g, owner],
                sib_part.at[g, n],
                part_send.at[g, n],
                part_recv.at[g, n],
                sib,
            )
    forward_frames()
    reduce_hop(groups - 1)
    loads[3].wait()
    make_target()
    for g in range(groups):
        part_copies[g, 1].wait_recv()
        hop_copies[g].wait_recv()
        pre_act = pre_v[g, me] + sib_part[g, 1] + cross_part[g].astype(jnp.float32)
        lift_v[pl.ds(g * sub, sub), :] = (pre_act / (1.0 + jnp.exp(-pre_act))).astype(
            jnp.bfloat16
        )

    def project(n, sums):
        cols = pl.ds(pl.multiple_of(n * tile, tile), tile)
        value = jnp.dot(lift_v[...], p2_v[:, cols], preferred_element_type=jnp.float32).astype(
            jnp.bfloat16
        )
        proj_out[:, cols] = value
        value = value.astype(jnp.float32)
        target = targ_out[:, cols]
        inner, proj_sq, target_sq = sums
        return (
            inner + jnp.sum(value * target, axis=-1, keepdims=True),
            proj_sq + jnp.sum(value * value, axis=-1, keepdims=True),
            target_sq + jnp.sum(target * target, axis=-1, keepdims=True),
        )

    zero = jnp.zeros((rows, 1), jnp.float32)
    inner, proj_sq, target_sq = lax.fori_loop(
        0, p2_v.shape[1] // tile, project, (zero, zero, zero)
    )
    cosine = inner / jnp.sqrt((proj_sq + 1e-06) * (target_sq + 1e-06))
    cos_out[...] = jnp.broadcast_to(cosine, (rows, rows)).T[0:1, :]

    for copy in hid_copies:
        copy.wait()
    for copies in (qkv_copies, att_copies, fwd_copies, part_copies, hop_copies):
        for copy in copies.values():
            copy.wait_send()
    for copy in dino_copies + frame_copies:
        copy.wait_send()


def place_kernel(hid, proj, targ, cos, hid_out, proj_out, targ_out, cos_out, hid_v, proj_v, targ_v, load_sem, store_sem):
    moves = [
        (hid.at[n, g], hid_v.at[n, g], hid_out.at[n, g])
        for n in range(hid.shape[0])
        for g in range(hid.shape[1])
    ]
    moves += [(proj, proj_v, proj_out), (targ, targ_v, targ_out)]
    loads = [
        pltpu.make_async_copy(src, held, load_sem.at[n]) for n, (src, held, _) in enumerate(moves)
    ]
    stores = [
        pltpu.make_async_copy(held, dst, store_sem.at[n]) for n, (_, held, dst) in enumerate(moves)
    ]
    for load in loads:
        load.start()
    cos_out[...] = cos[...]
    for load, store in zip(loads, stores):
        load.wait()
        store.start()
    for store in stores:
        store.wait()


def fused_device(
    query_rows,
    key_rows,
    value_rows,
    residual,
    out_weight,
    proj_first,
    proj_second,
    dino_feats,
    slot_frame,
    patch_taps,
):
    seq_count = lax.axis_size("seq")
    rows, all_cols = query_rows.shape
    tokens, wide = residual.shape
    units = proj_first.shape[1]
    feats = proj_second.shape[1]
    width = CHUNK_HEADS * HD
    chunks = all_cols // 4 // width
    groups = ROW_GROUPS
    sub = rows // groups
    held, part_patches = dino_feats.shape[:2]
    bf16 = jnp.bfloat16
    f32 = jnp.float32
    dma = pltpu.SemaphoreType.DMA
    any_spec = pl.BlockSpec(memory_space=pl.ANY)
    vmem_spec = pl.BlockSpec(memory_space=pltpu.VMEM)
    hidden, projected, target, cosine = pl.pallas_call(
        functools.partial(fused_kernel, seq_count),
        out_shape=(
            jax.ShapeDtypeStruct((4, groups, sub, wide), bf16),
            jax.ShapeDtypeStruct((rows, feats), bf16),
            jax.ShapeDtypeStruct((rows, feats), f32),
            jax.ShapeDtypeStruct((1, rows), f32),
        ),
        in_specs=[any_spec] * 8 + [pl.BlockSpec(memory_space=pltpu.SMEM), vmem_spec],
        out_specs=(any_spec, vmem_spec, vmem_spec, vmem_spec),
        scratch_shapes=[
            pltpu.VMEM((chunks, groups, 4, sub, width), bf16),
            pltpu.VMEM((2, chunks, tokens, width), bf16),
            pltpu.VMEM((groups, 4 * sub, all_cols), bf16),
            pltpu.VMEM((4 * sub, wide), f32),
            pltpu.VMEM(out_weight.shape, bf16),
            pltpu.VMEM(proj_first.shape, bf16),
            pltpu.VMEM(proj_second.shape, bf16),
            pltpu.VMEM((groups, 4, sub, wide), bf16),
            pltpu.VMEM((groups, 4, sub, wide), bf16),
            pltpu.VMEM((groups, 4, sub, units), f32),
            pltpu.VMEM((rows, units), bf16),
            pltpu.VMEM((groups, 2, sub, units), f32),
            pltpu.VMEM((groups, sub, units), bf16),
            pltpu.VMEM((groups, sub, units), bf16),
            pltpu.VMEM((seq_count, held, part_patches, feats), bf16),
            pltpu.VMEM((held, part_patches, feats), bf16),
            pltpu.VMEM((4, part_patches, feats), bf16),
            dma((4,)),
            dma((groups,)),
            dma((3, chunks)),
            dma((3, 3, chunks)),
            dma((3, 3, chunks)),
            dma((groups, 2)),
            dma((groups, 2)),
            dma((groups, 2)),
            dma((groups, 2)),
            dma((groups,)),
            dma((groups,)),
            dma((groups, 2)),
            dma((groups, 2)),
            dma((groups,)),
            dma((groups,)),
            dma((seq_count - 1,)),
            dma((seq_count - 1,)),
            dma((3,)),
            dma((3,)),
            dma((groups,)),
        ],
        compiler_params=pltpu.CompilerParams(
            collective_id=0, has_side_effects=True, vmem_limit_bytes=56 * 1024 * 1024
        ),
        cost_estimate=pl.CostEstimate(
            flops=2 * tokens * (all_cols * wide + wide * units),
            bytes_accessed=24 * 1024 * 1024,
            transcendentals=0,
        ),
        name="sublayer",
    )(
        query_rows.reshape(groups, sub, all_cols),
        key_rows,
        value_rows,
        residual.reshape(4, groups, sub, wide),
        out_weight,
        proj_first,
        proj_second,
        dino_feats,
        slot_frame,
        patch_taps.T,
    )
    parts = (hidden, projected, target, cosine)
    hidden, projected, target, cosine = pl.pallas_call(
        place_kernel,
        out_shape=tuple(jax.ShapeDtypeStruct(part.shape, part.dtype) for part in parts),
        in_specs=[any_spec] * 3 + [vmem_spec],
        out_specs=(any_spec,) * 3 + (vmem_spec,),
        scratch_shapes=[
            pltpu.VMEM(hidden.shape, bf16),
            pltpu.VMEM((rows, feats), bf16),
            pltpu.VMEM((rows, feats), f32),
            dma((4 * groups + 2,)),
            dma((4 * groups + 2,)),
        ],
        compiler_params=pltpu.CompilerParams(vmem_limit_bytes=56 * 1024 * 1024),
        name="place",
    )(*parts)
    return (hidden.reshape(tokens, wide), projected, target, cosine.reshape(rows))


def solution(mesh):
    body = fused_device if mesh.shape["head"] == 4 else per_device
    return jax.shard_map(
        body,
        mesh=mesh,
        in_specs=(
            P(("seq", "head"), None),
            P(("seq", "head"), None),
            P(("seq", "head"), None),
            P("seq", "head"),
            P(None, "head"),
            P("head", None),
            P(),
            P("seq", "head", None),
            P(),
            P(("seq", "head"), None),
        ),
        out_specs=(
            P("seq", "head"),
            P(("seq", "head"), None),
            P(("seq", "head"), None),
            P(("seq", "head")),
        ),
        check_vma=False,
    )
```
